512 devices in a mesh: dp: 64 (over y, x, core), rep: 8 (over z).
Axes of the slice: x: 4, y: 8, z: 8, core: 2. Of those that a mesh axis runs over, the one named last changes fastest.
Arguments:
- grad: bfloat16 [192, 720896], P('rep', 'dp'), parts along dimension 0, may hold values from -170 to 170
- momentum: float32 [192, 720896], P('rep', 'dp'), parts along dimension 0, may hold values from -340 to 340
- owners: int32 [192], P('rep'), parts along dimension 0, may hold values from 0 to 63, as said below
Outputs:
- new_momentum: float32 [192, 720896], P('rep', 'dp'), parts along dimension 0
- update: bfloat16 [192, 720896], P('rep', 'dp'), parts along dimension 0
- owned: bfloat16 [512, 704, 1024], P(('rep', 'dp')), parts along dimension 0
The draws below stay inside these ranges and needn't reach their ends.
There are 8 independent parts, one for each index of `rep`. The reference program is written for one: setup_inputs(seed, part) draws one part's arguments, and reference() takes and returns one part's arrays. A program takes and returns all parts, laid end to end along the dimension named above; each array names one. Nothing has to cross between parts.
Inputs may be any that keep to these rules, and one draw needn't show every extreme that they name: `owners`: no two matrices have the same owner.
All inputs are finite; a program needn't handle non-finite values.
Results may differ from the reference program's by a relative error of at most 0.007.
Values may be sent and summed in bfloat16 or wider, within the bound.
A program may use at most 64 MiB of HBM per device.

```python
import math
import jax
import jax.numpy as jnp
from jax import lax

R = 704
C = 1024
ITERS = 2
MATS = 24
N_DP = 64


def scales(key):
    row_key, col_key = jax.random.split(key)
    rows = jnp.exp(jax.random.uniform(row_key, (MATS, R, 1), jnp.float32, 0.0, math.log(10.0)))
    cols = jnp.exp(jax.random.uniform(col_key, (MATS, 1, C), jnp.float32, 0.0, math.log(10.0)))
    return rows * cols


def shaped(key, noise):
    left_key, right_key, spot_key, sign_key = jax.random.split(key, 4)
    left = jax.random.normal(left_key, (MATS, R, 32), jnp.float32)
    right = jax.random.normal(right_key, (MATS, 32, C), jnp.float32)
    shared = jnp.einsum('mrk,mkc->mrc', left, right, precision=lax.Precision.HIGHEST) / math.sqrt(32.0)
    dense = jnp.clip(shared + 0.3 * noise, -5.0, 5.0)
    spots = jax.random.randint(spot_key, (MATS, R, C), 0, 10000) == 0
    signs = jax.random.rademacher(sign_key, (MATS, R, C), jnp.float32)
    return jnp.where(spots, 5.0 * signs, 0.05 * dense)


def draw_grad(key, part):
    key = jax.random.fold_in(key, 11)
    base_key, noise_key, scale_key = jax.random.split(key, 3)
    noise = jax.random.normal(noise_key, (MATS, R, C), jnp.float32)
    values = shaped(base_key, noise) * scales(scale_key) / 3.0
    return values.reshape(MATS, R * C).astype(jnp.bfloat16)


def draw_momentum(key, part):
    key = jax.random.fold_in(key, 23)
    base_key, noise_key, scale_key = jax.random.split(key, 3)
    noise = jax.random.normal(noise_key, (MATS, R, C), jnp.float32)
    values = 2.0 * shaped(base_key, noise) * scales(scale_key) / 3.0
    return values.reshape(MATS, R * C).astype(jnp.float32)


def draw_owners(key, part):
    key = jax.random.fold_in(key, 5)
    first_key, second_key = jax.random.split(key)
    middle = jax.random.permutation(first_key, N_DP - 2).astype(jnp.int32) + 1
    ends = jnp.array([0, N_DP - 1], jnp.int32)
    chosen = jnp.concatenate([ends, middle[:MATS - 2]])
    return jax.random.permutation(second_key, chosen).astype(jnp.int32)


def setup_inputs(seed: int = 0, part: int = 0) -> dict:
    key_list = jax.random.split(jax.random.key(seed), 4)
    part_keys = jax.random.split(jax.random.fold_in(key_list[3], part), 4)
    grad = draw_grad(jax.random.fold_in(jax.random.fold_in(key_list[3], part), 71), part)
    momentum = draw_momentum(jax.random.fold_in(jax.random.fold_in(key_list[3], part), 71), part)
    owners = draw_owners(jax.random.fold_in(jax.random.fold_in(key_list[3], part), 71), part)
    return {"grad": grad, "momentum": momentum, "owners": owners}


MOMENTUM_RATE = 0.95
EPSILON = 1e-07
COEF_A = 3.4445
COEF_B = -4.775
COEF_C = 2.0315

def orthogonalize(matrix, norm):
    iterate = (matrix.astype(jnp.float32) / (norm + EPSILON)).astype(jnp.bfloat16)
    result = iterate.astype(jnp.float32)
    for step in range(ITERS):
        gram = jnp.dot(iterate, iterate.T, preferred_element_type=jnp.float32).astype(jnp.bfloat16)
        square = jnp.dot(gram, gram, preferred_element_type=jnp.float32)
        poly = (COEF_B * gram.astype(jnp.float32) + COEF_C * square).astype(jnp.bfloat16)
        result = COEF_A * iterate.astype(jnp.float32) + jnp.dot(poly, iterate, preferred_element_type=jnp.float32)
        if step + 1 < ITERS:
            iterate = result.astype(jnp.bfloat16)
    return (0.2 * math.sqrt(max(R, C)) * result).astype(jnp.bfloat16)

def one_matrix(matrix):
    norm = jnp.sqrt(jnp.sum(jnp.square(matrix.astype(jnp.float32))))
    return orthogonalize(matrix, norm)

def reference(grad, momentum, owners):
    grad_wide = grad.astype(jnp.float32)
    new_momentum = MOMENTUM_RATE * momentum + grad_wide
    nesterov = (grad_wide + MOMENTUM_RATE * new_momentum).astype(jnp.bfloat16)
    updates = lax.map(one_matrix, nesterov.reshape(MATS, R, C))
    owned = jnp.zeros((N_DP, R, C), jnp.bfloat16).at[owners.astype(jnp.int32)].set(updates)
    return (new_momentum, updates.reshape(MATS, R * C), owned)
```

```python
import math

import jax
import jax.numpy as jnp
from jax import lax
from jax.experimental import pallas as pl
from jax.experimental.pallas import tpu as pltpu
from jax.sharding import PartitionSpec as P

R = 704
C = 1024
RP = 768
MATS = 24
N = 64
T = 88
TILES = C // 128
FIXED = 24

MOMENTUM_RATE = 0.95
EPSILON = 1e-07
COEF_A = 3.4445
COEF_B = -4.775
COEF_C = 2.0315
SCALE = 0.2 * math.sqrt(max(R, C))
MESH = pl.DeviceIdType.MESH
NT = (((1,), (1,)), ((), ()))


def ring_offset(u):
    odd = u % 2
    return odd * ((u + 1) // 2) + (1 - odd) * (8 - u // 2)


def fixed_device(d):
    return 8 * (d // 3) + 3 * (d % 3)


def kernel(
    owners, grad, momentum,
    new_momentum, update, owned,
    table, has, place,
    flat, packed, send, held, x, x1, gram, poly, back, got,
    send_sem, recv_sem, back_sem, got_sem,
):
    me = lax.axis_index("dp")
    row, col = me // 8, me % 8
    is_fixed = col % 3 == 0
    mine = 3 * row + col // 3

    barrier = pltpu.get_barrier_semaphore()

    def greet(s, c):
        pl.semaphore_signal(barrier, inc=1, device_id={"dp": (me + s) % N}, device_id_type=MESH)
        return c

    lax.fori_loop(1, N, greet, 0)

    def step(t, c):
        columns = pl.ds(pl.multiple_of(t * 128, 128), 128)
        g = grad[:, columns].astype(jnp.float32)
        m = MOMENTUM_RATE * momentum[:, columns] + g
        new_momentum[:, columns] = m
        n = (g + MOMENTUM_RATE * m).astype(jnp.bfloat16).astype(jnp.float32)
        for kt in range(3):
            flat[pl.ds(pl.multiple_of(kt * 704 + t * 8, 8), 8), :] = n[8 * kt : 8 * kt + 8]
        return c

    lax.fori_loop(0, T, step, 0, unroll=4)

    for k in range(MATS):
        packed[k] = flat[pl.ds((k // 8) * 704 + k % 8, T, stride=8), :].astype(jnp.bfloat16)

    pl.semaphore_wait(barrier, N - 1)

    def deliver(p):
        send[p] = packed[table[p]]

        @pl.when(p == me)
        def _():
            pltpu.make_async_copy(send.at[p], held.at[p], recv_sem).start()

        @pl.when(p != me)
        def _():
            pltpu.make_async_remote_copy(
                send.at[p], held.at[me], send_sem, recv_sem, device_id={"dp": p}, device_id_type=MESH
            ).start()

    def to_fixed(s, c):
        there = (row + ring_offset(s // 3)) % 8
        deliver(8 * there + 3 * ((s + col) % 3))
        return c

    lax.fori_loop(0, FIXED, to_fixed, 0)

    def to_rest(s, c):
        there = (row + ring_offset(s // 5)) % 8
        i = (s + col) % 5
        deliver(8 * there + i + 1 + i // 2)
        return c

    lax.fori_loop(0, N - FIXED, to_rest, 0)

    pltpu.make_async_copy(held, held, recv_sem).wait()

    def unpack(q, total):
        block = held[q].astype(jnp.float32)
        flat[pl.ds(pl.multiple_of(q * T, 8), T), :] = block
        return total + jnp.sum((block * block).reshape(T // 8, 8, 128), axis=0)

    total = lax.fori_loop(0, N, unpack, jnp.zeros((8, 128), jnp.float32), unroll=2)
    inverse = 1.0 / (jnp.sqrt(jnp.sum(total)) + EPSILON)

    def normalize(i, c):
        rows = pl.ds(pl.multiple_of(i * 64, 64), 64)
        for t in range(TILES):
            part = flat[pl.ds(i * 512 + t, 64, stride=8), :]
            x[rows, 128 * t : 128 * t + 128] = (part * inverse).astype(jnp.bfloat16)
        return c

    lax.fori_loop(0, R // 64, normalize, 0)
    x[R:, :] = jnp.zeros((RP - R, C), jnp.bfloat16)

    def polynomial(source):
        @pl.loop(0, 3)
        def _(i):
            rows = pl.ds(pl.multiple_of(i * 256, 256), 256)
            gram[rows, :] = lax.dot_general(
                source[rows, :], source[...], NT, preferred_element_type=jnp.float32
            ).astype(jnp.bfloat16)

        @pl.loop(0, 3)
        def _(i):
            rows = pl.ds(pl.multiple_of(i * 256, 256), 256)
            here = gram[rows, :]
            square = jnp.dot(here, gram[...], preferred_element_type=jnp.float32)
            poly[rows, :] = (COEF_B * here.astype(jnp.float32) + COEF_C * square).astype(jnp.bfloat16)

    polynomial(x)

    @pl.loop(0, 3)
    def _(i):
        rows = pl.ds(pl.multiple_of(i * 256, 256), 256)
        y = COEF_A * x[rows, :].astype(jnp.float32) + jnp.dot(
            poly[rows, :], x[...], preferred_element_type=jnp.float32
        )
        x1[rows, :] = y.astype(jnp.bfloat16)

    polynomial(x1)
    owns = has[me] > 0

    for t in range(TILES // 2):
        columns = slice(256 * t, 256 * t + 256)
        z = SCALE * (
            COEF_A * x1[:R, columns].astype(jnp.float32)
            + jnp.dot(poly[:R, :], x1[:, columns], preferred_element_type=jnp.float32)
        )
        owned[0, :, columns] = jnp.where(owns, z, 0.0).astype(jnp.bfloat16)
        for h in range(2):
            flat[pl.ds(2 * t + h, R, stride=8), :] = z[:, 128 * h : 128 * h + 128]

    @pl.when(is_fixed)
    def _():
        def give(s, c):
            p = 8 * ((row + ring_offset(s // 8)) % 8) + (s + col) % 8
            back[p] = flat[pl.ds(pl.multiple_of(p * T, 8), T), :].astype(jnp.bfloat16)

            @pl.when(p == me)
            def _():
                pltpu.make_async_copy(back.at[p], got.at[mine], got_sem).start()

            @pl.when(p != me)
            def _():
                pltpu.make_async_remote_copy(
                    back.at[p], got.at[mine], back_sem, got_sem, device_id={"dp": p}, device_id_type=MESH
                ).start()

            return c

        lax.fori_loop(0, N, give, 0)

    sent = send.at[pl.ds(0, N - 1)]
    pltpu.make_async_copy(sent, sent, send_sem).wait()
    pltpu.make_async_copy(got, got, got_sem).wait()

    for k in range(MATS):
        flat[pl.ds((k // 8) * 704 + k % 8, T, stride=8), :] = got[place[k]].astype(jnp.float32)

    def write(t, c):
        columns = pl.ds(pl.multiple_of(t * 128, 128), 128)
        parts = [flat[pl.ds(pl.multiple_of(kt * 704 + t * 8, 8), 8), :] for kt in range(3)]
        update[:, columns] = jnp.concatenate(parts, axis=0).astype(jnp.bfloat16)
        return c

    lax.fori_loop(0, T, write, 0, unroll=4)

    @pl.when(is_fixed)
    def _():
        gone = back.at[pl.ds(0, N - 1)]
        pltpu.make_async_copy(gone, gone, back_sem).wait()


def plan_kernel(owners, table, has, place):
    def clear(p, c):
        table[p] = 0
        has[p] = 0
        return c

    lax.fori_loop(0, N, clear, 0, unroll=8)

    def own(k, c):
        p = owners[k]
        table[p] = k
        has[p] = 1
        return c

    lax.fori_loop(0, MATS, own, 0)

    def assign(k, d):
        p = owners[k]
        col = p % 8
        inside = col % 3 == 0

        def taken(d):
            return has[fixed_device(d)] == 1

        @pl.when(inside)
        def _():
            place[k] = 3 * (p // 8) + col // 3

        def outside():
            free = lax.while_loop(taken, lambda d: d + 1, d)
            place[k] = free
            table[fixed_device(free)] = k
            return free + 1

        return lax.cond(inside, lambda: d, outside)

    lax.fori_loop(0, MATS, assign, 0)


def body(grad, momentum, owners):
    smem = pl.BlockSpec(memory_space=pltpu.SMEM)
    vmem = pl.BlockSpec(memory_space=pltpu.VMEM)
    ints = lambda n: jax.ShapeDtypeStruct((n,), jnp.int32)
    table, has, place = pl.pallas_call(
        plan_kernel, out_shape=(ints(N), ints(N), ints(MATS)), in_specs=[smem], out_specs=(smem, smem, smem)
    )(owners)
    bf16, f32 = jnp.bfloat16, jnp.float32
    return pl.pallas_call(
        lambda table, has, place, g, m, *refs: kernel(None, g, m, *refs[:3], table, has, place, *refs[3:]),
        out_shape=(
            jax.ShapeDtypeStruct(momentum.shape, f32),
            jax.ShapeDtypeStruct(grad.shape, bf16),
            jax.ShapeDtypeStruct((1, R, C), bf16),
        ),
        in_specs=[smem, smem, smem, vmem, vmem],
        out_specs=(vmem, vmem, vmem),
        scratch_shapes=[
            pltpu.VMEM((N * T, 128), f32),
            pltpu.VMEM((MATS, T, 128), bf16),
            pltpu.VMEM((N, T, 128), bf16),
            pltpu.VMEM((N, T, 128), bf16),
            pltpu.VMEM((RP, C), bf16),
            pltpu.VMEM((RP, C), bf16),
            pltpu.VMEM((RP, RP), bf16),
            pltpu.VMEM((RP, RP), bf16),
            pltpu.VMEM((N, T, 128), bf16),
            pltpu.VMEM((FIXED, T, 128), bf16),
            pltpu.SemaphoreType.DMA,
            pltpu.SemaphoreType.DMA,
            pltpu.SemaphoreType.DMA,
            pltpu.SemaphoreType.DMA,
        ],
        compiler_params=pltpu.CompilerParams(
            collective_id=0, has_side_effects=True, vmem_limit_bytes=48 << 20
        ),
    )(table, has, place, grad, momentum)


def solution(mesh):
    return jax.shard_map(
        body,
        mesh=mesh,
        in_specs=(P("rep", "dp"), P("rep", "dp"), P("rep")),
        out_specs=(P("rep", "dp"), P("rep", "dp"), P(("rep", "dp"), None, None)),
        check_vma=False,
    )
```

```python
import math

import jax
import jax.numpy as jnp
from jax import lax
from jax.experimental import pallas as pl
from jax.experimental.pallas import tpu as pltpu
from jax.sharding import PartitionSpec as P

R = 704
C = 1024
RP = 768
MATS = 24
N = 64
T = 88
TILES = C // 128
PARTS = 4
PREPARE_MIB = 53
FIXED = 24

MOMENTUM_RATE = 0.95
EPSILON = 1e-07
COEF_A = 3.4445
COEF_B = -4.775
COEF_C = 2.0315
SCALE = 0.2 * math.sqrt(max(R, C))
MESH = pl.DeviceIdType.MESH
NT = (((1,), (1,)), ((), ()))


def ring_offset(u):
    v = 7 - u
    odd = v % 2
    return odd * ((v + 1) // 2) + (1 - odd) * (8 - v // 2)


def fixed_device(d):
    row = d // 3
    return 8 * row + (3 * (d % 3) + 6 * row) % 8


def other_device(row, i):
    return 8 * row + (i + 1 + i // 2 + 6 * row) % 8


def prepare_kernel(
    owners_hbm, grad_hbm, momentum_hbm,
    new_momentum_hbm, packed, plan,
    owners, grad, momentum, flat, load_sem, store_sem,
):
    width = grad.shape[1] // PARTS

    def load(i):
        columns = pl.ds(i * width, width)
        return (
            pltpu.make_async_copy(grad_hbm.at[:, columns], grad.at[:, columns], load_sem.at[2 * i]),
            pltpu.make_async_copy(momentum_hbm.at[:, columns], momentum.at[:, columns], load_sem.at[2 * i + 1]),
        )

    def store(i):
        columns = pl.ds(i * width, width)
        return pltpu.make_async_copy(momentum.at[:, columns], new_momentum_hbm.at[:, columns], store_sem.at[i])

    whose = pltpu.make_async_copy(owners_hbm, owners, load_sem.at[2 * PARTS])
    whose.start()
    for i in range(PARTS):
        for copy in load(i):
            copy.start()

    whose.wait()
    lane = lax.broadcasted_iota(jnp.int32, (8, 128), 1)
    matrix = jnp.zeros((8, 128), jnp.int32)
    owning = jnp.zeros((8, 128), jnp.int32)
    for k in range(MATS):
        here = lane == owners[k]
        matrix = jnp.where(here, k, matrix)
        owning = jnp.where(here, 1, owning)
    in_fixed = lambda c: (c == 0) | (c == 3) | (c == 6)
    free = in_fixed((lane + 2 * (lane // 8)) & 7) & (lane < N) & (owning == 0)
    rank = jnp.where(free, 1, 0)
    for shift in (1, 2, 4, 8, 16, 32):
        rank = rank + jnp.where(lane >= shift, pltpu.roll(rank, shift, 1), 0)
    rank = jnp.where(free, rank, 0)
    count = jnp.int32(0)
    for k in range(MATS):
        outside = jnp.where(in_fixed((owners[k] + 2 * (owners[k] // 8)) & 7), 0, 1)
        count = count + outside
        matrix = jnp.where(rank == count * outside + (outside - 1), k, matrix)
    plan[0] = matrix
    plan[1] = owning

    for i in range(PARTS):
        for copy in load(i):
            copy.wait()

        def step(t, c):
            columns = pl.ds(pl.multiple_of(t * 128, 128), 128)
            g = grad[:, columns].astype(jnp.float32)
            m = MOMENTUM_RATE * momentum[:, columns] + g
            momentum[:, columns] = m
            n = (g + MOMENTUM_RATE * m).astype(jnp.bfloat16).astype(jnp.float32)
            for kt in range(3):
                flat[pl.ds(pl.multiple_of(kt * 704 + t * 8, 8), 8), :] = n[8 * kt : 8 * kt + 8]
            return c

        lax.fori_loop(i * T // PARTS, (i + 1) * T // PARTS, step, 0, unroll=11)
        store(i).start()

    for k in range(MATS):
        packed[k] = flat[pl.ds((k // 8) * 704 + k % 8, T, stride=8), :].astype(jnp.bfloat16)
    for i in range(PARTS):
        store(i).wait()


def kernel(
    plan, packed,
    update, owned,
    table, place,
    flat, send, held, x, x1, gram, poly, back, got,
    load_sem, send_sem, recv_sem, back_sem, got_sem,
):
    me = lax.axis_index("dp")
    row, col = me // 8, me % 8
    turned = (col + 2 * row) % 8
    is_fixed = turned % 3 == 0
    mine = 3 * row + turned // 3

    pltpu.make_async_copy(plan, table, load_sem).start()
    barrier = pltpu.get_barrier_semaphore()

    def greet(s, c):
        pl.semaphore_signal(barrier, inc=1, device_id={"dp": (me + s) % N}, device_id_type=MESH)
        return c

    lax.fori_loop(1, N, greet, 0)
    pltpu.make_async_copy(plan, table, load_sem).wait()
    pl.semaphore_wait(barrier, N - 1)

    def deliver(p):
        send[p] = packed[table[0, 0, p]]

        @pl.when(p == me)
        def _():
            pltpu.make_async_copy(send.at[p], held.at[p], recv_sem).start()

        @pl.when(p != me)
        def _():
            pltpu.make_async_remote_copy(
                send.at[p], held.at[me], send_sem, recv_sem, device_id={"dp": p}, device_id_type=MESH
            ).start()

    def to_fixed(s, c):
        there = (row + ring_offset(s % 8)) % 8
        deliver(fixed_device(3 * there + (s // 8 + col) % 3))
        return c

    lax.fori_loop(0, FIXED, to_fixed, 0)

    def to_rest(s, c):
        there = (row + ring_offset(s % 8)) % 8
        deliver(other_device(there, (s // 8 + col) % 5))
        return c

    lax.fori_loop(0, N - FIXED, to_rest, 0)

    def find(k, c):
        where = jnp.int32(0)
        for d in range(FIXED):
            where = jnp.where(table[0, 0, fixed_device(d)] == k, d, where)
        place[k] = where
        return c

    lax.fori_loop(0, MATS, find, 0)

    pltpu.make_async_copy(held, held, recv_sem).wait()

    def unpack(q, total):
        block = held[q].astype(jnp.float32)
        flat[pl.ds(pl.multiple_of(q * T, 8), T), :] = block
        return total + jnp.sum((block * block).reshape(T // 8, 8, 128), axis=0)

    total = lax.fori_loop(0, N, unpack, jnp.zeros((8, 128), jnp.float32), unroll=2)
    inverse = 1.0 / (jnp.sqrt(jnp.sum(total)) + EPSILON)

    def normalize(i, c):
        rows = pl.ds(pl.multiple_of(i * 64, 64), 64)
        for t in range(TILES):
            part = flat[pl.ds(i * 512 + t, 64, stride=8), :]
            x[rows, 128 * t : 128 * t + 128] = (part * inverse).astype(jnp.bfloat16)
        return c

    lax.fori_loop(0, R // 64, normalize, 0)
    x[R:, :] = jnp.zeros((RP - R, C), jnp.bfloat16)

    def polynomial(source):
        @pl.loop(0, 3)
        def _(i):
            rows = pl.ds(pl.multiple_of(i * 256, 256), 256)
            gram[rows, :] = lax.dot_general(
                source[rows, :], source[...], NT, preferred_element_type=jnp.float32
            ).astype(jnp.bfloat16)

        @pl.loop(0, 3)
        def _(i):
            rows = pl.ds(pl.multiple_of(i * 256, 256), 256)
            here = gram[rows, :]
            square = jnp.dot(here, gram[...], preferred_element_type=jnp.float32)
            poly[rows, :] = (COEF_B * here.astype(jnp.float32) + COEF_C * square).astype(jnp.bfloat16)

    polynomial(x)

    @pl.loop(0, 3)
    def _(i):
        rows = pl.ds(pl.multiple_of(i * 256, 256), 256)
        y = COEF_A * x[rows, :].astype(jnp.float32) + jnp.dot(
            poly[rows, :], x[...], preferred_element_type=jnp.float32
        )
        x1[rows, :] = y.astype(jnp.bfloat16)

    polynomial(x1)
    owns = table[1, 0, me] > 0

    for t in range(TILES // 2):
        columns = slice(256 * t, 256 * t + 256)
        z = SCALE * (
            COEF_A * x1[:R, columns].astype(jnp.float32)
            + jnp.dot(poly[:R, :], x1[:, columns], preferred_element_type=jnp.float32)
        )
        owned[0, :, columns] = jnp.where(owns, z, 0.0).astype(jnp.bfloat16)
        for h in range(2):
            flat[pl.ds(2 * t + h, R, stride=8), :] = z[:, 128 * h : 128 * h + 128]

    @pl.when(is_fixed)
    def _():
        def give(s, c):
            p = 8 * ((row + ring_offset(s % 8)) % 8) + (s // 8 + col) % 8
            back[p] = flat[pl.ds(pl.multiple_of(p * T, 8), T), :].astype(jnp.bfloat16)

            @pl.when(p == me)
            def _():
                pltpu.make_async_copy(back.at[p], got.at[mine], got_sem).start()

            @pl.when(p != me)
            def _():
                pltpu.make_async_remote_copy(
                    back.at[p], got.at[mine], back_sem, got_sem, device_id={"dp": p}, device_id_type=MESH
                ).start()

            return c

        lax.fori_loop(0, N, give, 0)

    sent = send.at[pl.ds(0, N - 1)]
    pltpu.make_async_copy(sent, sent, send_sem).wait()
    pltpu.make_async_copy(got, got, got_sem).wait()

    for k in range(MATS):
        flat[pl.ds((k // 8) * 704 + k % 8, T, stride=8), :] = got[place[k]].astype(jnp.float32)

    def write(t, c):
        columns = pl.ds(pl.multiple_of(t * 128, 128), 128)
        parts = [flat[pl.ds(pl.multiple_of(kt * 704 + t * 8, 8), 8), :] for kt in range(3)]
        update[:, columns] = jnp.concatenate(parts, axis=0).astype(jnp.bfloat16)
        return c

    lax.fori_loop(0, T, write, 0, unroll=4)

    @pl.when(is_fixed)
    def _():
        gone = back.at[pl.ds(0, N - 1)]
        pltpu.make_async_copy(gone, gone, back_sem).wait()


def write_kernel(update, owned, update_hbm, owned_hbm, sems):
    copies = [
        pltpu.make_async_copy(update, update_hbm, sems.at[0]),
        pltpu.make_async_copy(owned, owned_hbm, sems.at[1]),
    ]
    for copy in copies:
        copy.start()
    for copy in copies:
        copy.wait()


def body(grad, momentum, owners):
    hbm = pl.BlockSpec(memory_space=pltpu.HBM)
    vmem = pl.BlockSpec(memory_space=pltpu.VMEM)
    bf16, f32, i32 = jnp.bfloat16, jnp.float32, jnp.int32
    shapes = (jax.ShapeDtypeStruct(grad.shape, bf16), jax.ShapeDtypeStruct((1, R, C), bf16))
    new_momentum, packed, plan = pl.pallas_call(
        prepare_kernel,
        out_shape=(
            jax.ShapeDtypeStruct(momentum.shape, f32),
            jax.ShapeDtypeStruct((MATS, T, 128), bf16),
            jax.ShapeDtypeStruct((2, 8, 128), i32),
        ),
        in_specs=[hbm, hbm, hbm],
        out_specs=(hbm, vmem, vmem),
        scratch_shapes=[
            pltpu.SMEM((MATS,), i32),
            pltpu.VMEM(grad.shape, bf16),
            pltpu.VMEM(momentum.shape, f32),
            pltpu.VMEM((MATS * T, 128), f32),
            pltpu.SemaphoreType.DMA((2 * PARTS + 1,)),
            pltpu.SemaphoreType.DMA((PARTS,)),
        ],
        compiler_params=pltpu.CompilerParams(vmem_limit_bytes=PREPARE_MIB << 20),
    )(owners, grad, momentum)
    results = pl.pallas_call(
        kernel,
        out_shape=shapes,
        in_specs=[vmem, vmem],
        out_specs=(vmem, vmem),
        scratch_shapes=[
            pltpu.SMEM((2, 8, 128), i32),
            pltpu.SMEM((MATS,), i32),
            pltpu.VMEM((N * T, 128), f32),
            pltpu.VMEM((N, T, 128), bf16),
            pltpu.VMEM((N, T, 128), bf16),
            pltpu.VMEM((RP, C), bf16),
            pltpu.VMEM((RP, C), bf16),
            pltpu.VMEM((RP, RP), bf16),
            pltpu.VMEM((RP, RP), bf16),
            pltpu.VMEM((N, T, 128), bf16),
            pltpu.VMEM((FIXED, T, 128), bf16),
            pltpu.SemaphoreType.DMA,
            pltpu.SemaphoreType.DMA,
            pltpu.SemaphoreType.DMA,
            pltpu.SemaphoreType.DMA,
            pltpu.SemaphoreType.DMA,
        ],
        compiler_params=pltpu.CompilerParams(
            collective_id=0, has_side_effects=True, vmem_limit_bytes=44 << 20
        ),
    )(plan, packed)
    update, owned = pl.pallas_call(
        write_kernel,
        out_shape=shapes,
        in_specs=[vmem, vmem],
        out_specs=(hbm, hbm),
        scratch_shapes=[pltpu.SemaphoreType.DMA((2,))],
        compiler_params=pltpu.CompilerParams(vmem_limit_bytes=4 << 20),
    )(*results)
    return new_momentum, update, owned


def solution(mesh):
    return jax.shard_map(
        body,
        mesh=mesh,
        in_specs=(P("rep", "dp"), P("rep", "dp"), P("rep")),
        out_specs=(P("rep", "dp"), P("rep", "dp"), P(("rep", "dp"), None, None)),
        check_vma=False,
    )
```

```python
import math

import jax
import jax.numpy as jnp
from jax import lax
from jax.experimental import pallas as pl
from jax.experimental.pallas import tpu as pltpu
from jax.sharding import PartitionSpec as P

R = 704
C = 1024
RP = 768
MATS = 24
N = 64
T = 88
TILES = C // 128
PARTS = 4
PREPARE_MIB = 53
FIXED = 24

MOMENTUM_RATE = 0.95
EPSILON = 1e-07
COEF_A = 3.4445
COEF_B = -4.775
COEF_C = 2.0315
SCALE = 0.2 * math.sqrt(max(R, C))
MESH = pl.DeviceIdType.MESH
NT = (((1,), (1,)), ((), ()))


def ring_offset(u):
    v = 7 - u
    odd = v % 2
    return odd * ((v + 1) // 2) + (1 - odd) * (8 - v // 2)


def fixed_device(d):
    row = d // 3
    return 8 * row + (3 * (d % 3) + 6 * row) % 8


def other_device(row, i):
    return 8 * row + (i + 1 + i // 2 + 6 * row) % 8


def prepare_kernel(
    owners_hbm, grad_hbm, momentum_hbm,
    new_momentum_hbm, packed, plan,
    owners, grad, momentum, flat, load_sem, store_sem,
):
    width = grad.shape[1] // PARTS

    def load(i):
        columns = pl.ds(i * width, width)
        return (
            pltpu.make_async_copy(grad_hbm.at[:, columns], grad.at[:, columns], load_sem.at[2 * i]),
            pltpu.make_async_copy(momentum_hbm.at[:, columns], momentum.at[:, columns], load_sem.at[2 * i + 1]),
        )

    def store(i):
        columns = pl.ds(i * width, width)
        return pltpu.make_async_copy(momentum.at[:, columns], new_momentum_hbm.at[:, columns], store_sem.at[i])

    whose = pltpu.make_async_copy(owners_hbm, owners, load_sem.at[2 * PARTS])
    whose.start()
    for i in range(PARTS):
        for copy in load(i):
            copy.start()

    whose.wait()
    lane = lax.broadcasted_iota(jnp.int32, (8, 128), 1)
    matrix = jnp.zeros((8, 128), jnp.int32)
    owning = jnp.zeros((8, 128), jnp.int32)
    for k in range(MATS):
        here = lane == owners[k]
        matrix = jnp.where(here, k, matrix)
        owning = jnp.where(here, 1, owning)
    in_fixed = lambda c: (c == 0) | (c == 3) | (c == 6)
    free = in_fixed((lane + 2 * (lane // 8)) & 7) & (lane < N) & (owning == 0)
    rank = jnp.where(free, 1, 0)
    for shift in (1, 2, 4, 8, 16, 32):
        rank = rank + jnp.where(lane >= shift, pltpu.roll(rank, shift, 1), 0)
    rank = jnp.where(free, rank, 0)
    count = jnp.int32(0)
    for k in range(MATS):
        outside = jnp.where(in_fixed((owners[k] + 2 * (owners[k] // 8)) & 7), 0, 1)
        count = count + outside
        matrix = jnp.where(rank == count * outside + (outside - 1), k, matrix)
    plan[0] = matrix
    plan[1] = owning

    for i in range(PARTS):
        for copy in load(i):
            copy.wait()

        def step(t, c):
            columns = pl.ds(pl.multiple_of(t * 128, 128), 128)
            g = grad[:, columns].astype(jnp.float32)
            m = MOMENTUM_RATE * momentum[:, columns] + g
            momentum[:, columns] = m
            n = (g + MOMENTUM_RATE * m).astype(jnp.bfloat16).astype(jnp.float32)
            for kt in range(3):
                flat[pl.ds(pl.multiple_of(kt * 704 + t * 8, 8), 8), :] = n[8 * kt : 8 * kt + 8]
            return c

        lax.fori_loop(i * T // PARTS, (i + 1) * T // PARTS, step, 0, unroll=11)
        store(i).start()

    for k in range(MATS):
        packed[k] = flat[pl.ds((k // 8) * 704 + k % 8, T, stride=8), :].astype(jnp.bfloat16)
    for i in range(PARTS):
        store(i).wait()


def kernel(
    plan, packed,
    update, owned,
    table, place,
    flat, send, held, x, x1, gram, poly, back, got,
    load_sem, met_sem, send_sem, recv_sem, back_sem, got_sem,
):
    me = lax.axis_index("dp")
    row, col = me // 8, me % 8
    turned = (col + 2 * row) % 8
    is_fixed = turned % 3 == 0
    mine = 3 * row + turned // 3

    pltpu.make_async_copy(plan, table, load_sem).start()
    barrier = pltpu.get_barrier_semaphore()

    def greet(s, c):
        there = 8 * ((row + s) % 8) + col
        pl.semaphore_signal(barrier, inc=1, device_id={"dp": there}, device_id_type=MESH)
        there = 8 * row + (col + s) % 8
        pl.semaphore_signal(barrier, inc=1, device_id={"dp": there}, device_id_type=MESH)
        return c

    lax.fori_loop(1, 8, greet, 0, unroll=True)
    pltpu.make_async_copy(plan, table, load_sem).wait()
    pl.semaphore_wait(barrier, 14)

    def announce(s, c):
        there = 8 * ((row + s) % 8) + col
        pl.semaphore_signal(met_sem, inc=1, device_id={"dp": there}, device_id_type=MESH)
        return c

    lax.fori_loop(1, 8, announce, 0, unroll=True)

    def deliver(p):
        send[p] = packed[table[0, 0, p]]

        @pl.when(p == me)
        def _():
            pltpu.make_async_copy(send.at[p], held.at[p], recv_sem).start()

        @pl.when(p != me)
        def _():
            pltpu.make_async_remote_copy(
                send.at[p], held.at[me], send_sem, recv_sem, device_id={"dp": p}, device_id_type=MESH
            ).start()

    def to_column(s, c):
        deliver(8 * ((row + ring_offset(s)) % 8) + col)
        return c

    lax.fori_loop(0, 7, to_column, 0)
    pl.semaphore_wait(met_sem, 7)

    def deliver_outside(p):
        @pl.when((p % 8 != col) | (p == me))
        def _():
            deliver(p)

    def to_fixed(s, c):
        there = (row + ring_offset(s % 8)) % 8
        deliver_outside(fixed_device(3 * there + (s // 8 + col) % 3))
        return c

    lax.fori_loop(0, FIXED, to_fixed, 0)

    def to_rest(s, c):
        there = (row + ring_offset(s % 8)) % 8
        deliver_outside(other_device(there, (s // 8 + col) % 5))
        return c

    lax.fori_loop(0, N - FIXED, to_rest, 0)

    def find(k, c):
        where = jnp.int32(0)
        for d in range(FIXED):
            where = jnp.where(table[0, 0, fixed_device(d)] == k, d, where)
        place[k] = where
        return c

    lax.fori_loop(0, MATS, find, 0)

    pltpu.make_async_copy(held, held, recv_sem).wait()

    def unpack(q, total):
        block = held[q].astype(jnp.float32)
        flat[pl.ds(pl.multiple_of(q * T, 8), T), :] = block
        return total + jnp.sum((block * block).reshape(T // 8, 8, 128), axis=0)

    total = lax.fori_loop(0, N, unpack, jnp.zeros((8, 128), jnp.float32), unroll=2)
    inverse = 1.0 / (jnp.sqrt(jnp.sum(total)) + EPSILON)

    def normalize(i, c):
        rows = pl.ds(pl.multiple_of(i * 64, 64), 64)
        for t in range(TILES):
            part = flat[pl.ds(i * 512 + t, 64, stride=8), :]
            x[rows, 128 * t : 128 * t + 128] = (part * inverse).astype(jnp.bfloat16)
        return c

    lax.fori_loop(0, R // 64, normalize, 0)
    x[R:, :] = jnp.zeros((RP - R, C), jnp.bfloat16)

    def polynomial(source):
        @pl.loop(0, 3)
        def _(i):
            rows = pl.ds(pl.multiple_of(i * 256, 256), 256)
            gram[rows, :] = lax.dot_general(
                source[rows, :], source[...], NT, preferred_element_type=jnp.float32
            ).astype(jnp.bfloat16)

        @pl.loop(0, 3)
        def _(i):
            rows = pl.ds(pl.multiple_of(i * 256, 256), 256)
            here = gram[rows, :]
            square = jnp.dot(here, gram[...], preferred_element_type=jnp.float32)
            poly[rows, :] = (COEF_B * here.astype(jnp.float32) + COEF_C * square).astype(jnp.bfloat16)

    polynomial(x)

    @pl.loop(0, 3)
    def _(i):
        rows = pl.ds(pl.multiple_of(i * 256, 256), 256)
        y = COEF_A * x[rows, :].astype(jnp.float32) + jnp.dot(
            poly[rows, :], x[...], preferred_element_type=jnp.float32
        )
        x1[rows, :] = y.astype(jnp.bfloat16)

    polynomial(x1)
    owns = table[1, 0, me] > 0

    for t in range(TILES // 2):
        columns = slice(256 * t, 256 * t + 256)
        z = SCALE * (
            COEF_A * x1[:R, columns].astype(jnp.float32)
            + jnp.dot(poly[:R, :], x1[:, columns], preferred_element_type=jnp.float32)
        )
        owned[0, :, columns] = jnp.where(owns, z, 0.0).astype(jnp.bfloat16)
        for h in range(2):
            flat[pl.ds(2 * t + h, R, stride=8), :] = z[:, 128 * h : 128 * h + 128]

    @pl.when(is_fixed)
    def _():
        def give(s, c):
            p = 8 * ((row + ring_offset(s % 8)) % 8) + (s // 8 + col) % 8
            back[p] = flat[pl.ds(pl.multiple_of(p * T, 8), T), :].astype(jnp.bfloat16)

            @pl.when(p == me)
            def _():
                pltpu.make_async_copy(back.at[p], got.at[mine], got_sem).start()

            @pl.when(p != me)
            def _():
                pltpu.make_async_remote_copy(
                    back.at[p], got.at[mine], back_sem, got_sem, device_id={"dp": p}, device_id_type=MESH
                ).start()

            return c

        lax.fori_loop(0, N, give, 0)

    sent = send.at[pl.ds(0, N - 1)]
    pltpu.make_async_copy(sent, sent, send_sem).wait()
    pltpu.make_async_copy(got, got, got_sem).wait()

    for k in range(MATS):
        flat[pl.ds((k // 8) * 704 + k % 8, T, stride=8), :] = got[place[k]].astype(jnp.float32)

    def write(t, c):
        columns = pl.ds(pl.multiple_of(t * 128, 128), 128)
        parts = [flat[pl.ds(pl.multiple_of(kt * 704 + t * 8, 8), 8), :] for kt in range(3)]
        update[:, columns] = jnp.concatenate(parts, axis=0).astype(jnp.bfloat16)
        return c

    lax.fori_loop(0, T, write, 0, unroll=4)

    @pl.when(is_fixed)
    def _():
        gone = back.at[pl.ds(0, N - 1)]
        pltpu.make_async_copy(gone, gone, back_sem).wait()


def write_kernel(update, owned, update_hbm, owned_hbm, sems):
    copies = [
        pltpu.make_async_copy(update, update_hbm, sems.at[0]),
        pltpu.make_async_copy(owned, owned_hbm, sems.at[1]),
    ]
    for copy in copies:
        copy.start()
    for copy in copies:
        copy.wait()


def body(grad, momentum, owners):
    hbm = pl.BlockSpec(memory_space=pltpu.HBM)
    vmem = pl.BlockSpec(memory_space=pltpu.VMEM)
    bf16, f32, i32 = jnp.bfloat16, jnp.float32, jnp.int32
    shapes = (jax.ShapeDtypeStruct(grad.shape, bf16), jax.ShapeDtypeStruct((1, R, C), bf16))
    new_momentum, packed, plan = pl.pallas_call(
        prepare_kernel,
        out_shape=(
            jax.ShapeDtypeStruct(momentum.shape, f32),
            jax.ShapeDtypeStruct((MATS, T, 128), bf16),
            jax.ShapeDtypeStruct((2, 8, 128), i32),
        ),
        in_specs=[hbm, hbm, hbm],
        out_specs=(hbm, vmem, vmem),
        scratch_shapes=[
            pltpu.SMEM((MATS,), i32),
            pltpu.VMEM(grad.shape, bf16),
            pltpu.VMEM(momentum.shape, f32),
            pltpu.VMEM((MATS * T, 128), f32),
            pltpu.SemaphoreType.DMA((2 * PARTS + 1,)),
            pltpu.SemaphoreType.DMA((PARTS,)),
        ],
        compiler_params=pltpu.CompilerParams(vmem_limit_bytes=PREPARE_MIB << 20),
    )(owners, grad, momentum)
    results = pl.pallas_call(
        kernel,
        out_shape=shapes,
        in_specs=[vmem, vmem],
        out_specs=(vmem, vmem),
        scratch_shapes=[
            pltpu.SMEM((2, 8, 128), i32),
            pltpu.SMEM((MATS,), i32),
            pltpu.VMEM((N * T, 128), f32),
            pltpu.VMEM((N, T, 128), bf16),
            pltpu.VMEM((N, T, 128), bf16),
            pltpu.VMEM((RP, C), bf16),
            pltpu.VMEM((RP, C), bf16),
            pltpu.VMEM((RP, RP), bf16),
            pltpu.VMEM((RP, RP), bf16),
            pltpu.VMEM((N, T, 128), bf16),
            pltpu.VMEM((FIXED, T, 128), bf16),
            pltpu.SemaphoreType.DMA,
            pltpu.SemaphoreType.REGULAR,
            pltpu.SemaphoreType.DMA,
            pltpu.SemaphoreType.DMA,
            pltpu.SemaphoreType.DMA,
            pltpu.SemaphoreType.DMA,
        ],
        compiler_params=pltpu.CompilerParams(
            collective_id=0, has_side_effects=True, vmem_limit_bytes=44 << 20
        ),
    )(plan, packed)
    update, owned = pl.pallas_call(
        write_kernel,
        out_shape=shapes,
        in_specs=[vmem, vmem],
        out_specs=(hbm, hbm),
        scratch_shapes=[pltpu.SemaphoreType.DMA((2,))],
        compiler_params=pltpu.CompilerParams(vmem_limit_bytes=4 << 20),
    )(*results)
    return new_momentum, update, owned


def solution(mesh):
    return jax.shard_map(
        body,
        mesh=mesh,
        in_specs=(P("rep", "dp"), P("rep", "dp"), P("rep")),
        out_specs=(P("rep", "dp"), P("rep", "dp"), P(("rep", "dp"), None, None)),
        check_vma=False,
    )
```

```python
import math

import jax
import jax.numpy as jnp
from jax import lax
from jax.experimental import pallas as pl
from jax.experimental.pallas import tpu as pltpu
from jax.sharding import PartitionSpec as P

R = 704
C = 1024
RP = 768
MATS = 24
N = 64
T = 88
TILES = C // 128
PARTS = ((0, 30), (30, 30), (60, 28))
ROWS = ((0, 240), (240, 240), (480, 224))
MAIN_KIB = 52000
FIXED = 24

MOMENTUM_RATE = 0.95
EPSILON = 1e-07
COEF_A = 3.4445
COEF_B = -4.775
COEF_C = 2.0315
SCALE = 0.2 * math.sqrt(max(R, C))
MESH = pl.DeviceIdType.MESH
NT = (((1,), (1,)), ((), ()))


def ring_offset(u):
    v = 7 - u
    odd = v % 2
    return odd * ((v + 1) // 2) + (1 - odd) * (8 - v // 2)


def fixed_device(d):
    row = d // 3
    return 8 * row + (3 * (d % 3) + 6 * row) % 8


def other_device(row, i):
    return 8 * row + (i + 1 + i // 2 + 6 * row) % 8


def kernel(
    owners_hbm, grad_hbm, momentum_hbm,
    *refs,
):
    new_momentum, update, owned = refs[0:3], refs[3:6], refs[6:9]
    (
        owners, grad, momentum, plan, packed, table, place,
        flat, send, held, x, x1, gram, poly, back, got,
        load_sem, met_sem, send_sem, recv_sem, back_sem, got_sem,
    ) = refs[9:]
    me = lax.axis_index("dp")
    row, col = me // 8, me % 8
    turned = (col + 2 * row) % 8
    is_fixed = turned % 3 == 0
    mine = 3 * row + turned // 3

    def load(i):
        columns = pl.ds(128 * PARTS[i][0], 128 * PARTS[i][1])
        return (
            pltpu.make_async_copy(grad_hbm.at[:, columns], grad.at[:, columns], load_sem.at[2 * i]),
            pltpu.make_async_copy(momentum_hbm.at[:, columns], momentum.at[:, columns], load_sem.at[2 * i + 1]),
        )

    whose = pltpu.make_async_copy(owners_hbm, owners, load_sem.at[2 * len(PARTS)])
    planned = pltpu.make_async_copy(plan, table, load_sem.at[2 * len(PARTS)])
    whose.start()
    for i in range(len(PARTS)):
        for copy in load(i):
            copy.start()

    barrier = pltpu.get_barrier_semaphore()

    def greet(s, c):
        there = 8 * ((row + s) % 8) + col
        pl.semaphore_signal(barrier, inc=1, device_id={"dp": there}, device_id_type=MESH)
        there = 8 * row + (col + s) % 8
        pl.semaphore_signal(barrier, inc=1, device_id={"dp": there}, device_id_type=MESH)
        return c

    lax.fori_loop(1, 8, greet, 0, unroll=True)
    whose.wait()
    lane = lax.broadcasted_iota(jnp.int32, (8, 128), 1)
    matrix = jnp.zeros((8, 128), jnp.int32)
    owning = jnp.zeros((8, 128), jnp.int32)
    for k in range(MATS):
        here = lane == owners[k]
        matrix = jnp.where(here, k, matrix)
        owning = jnp.where(here, 1, owning)
    in_fixed = lambda c: (c == 0) | (c == 3) | (c == 6)
    free = in_fixed((lane + 2 * (lane // 8)) & 7) & (lane < N) & (owning == 0)
    rank = jnp.where(free, 1, 0)
    for shift in (1, 2, 4, 8, 16, 32):
        rank = rank + jnp.where(lane >= shift, pltpu.roll(rank, shift, 1), 0)
    rank = jnp.where(free, rank, 0)
    count = jnp.int32(0)
    for k in range(MATS):
        outside = jnp.where(in_fixed((owners[k] + 2 * (owners[k] // 8)) & 7), 0, 1)
        count = count + outside
        matrix = jnp.where(rank == count * outside + (outside - 1), k, matrix)
    plan[0] = matrix
    plan[1] = owning

    planned.start()

    for i, (first, count) in enumerate(PARTS):
        for copy in load(i):
            copy.wait()

        def step(t, c):
            columns = pl.ds(pl.multiple_of(t * 128, 128), 128)
            g = grad[:, columns].astype(jnp.float32)
            m = MOMENTUM_RATE * momentum[:, columns] + g
            new_momentum[i][:, pl.ds(pl.multiple_of((t - first) * 128, 128), 128)] = m
            n = (g + MOMENTUM_RATE * m).astype(jnp.bfloat16).astype(jnp.float32)
            for kt in range(3):
                flat[pl.ds(pl.multiple_of(kt * 704 + t * 8, 8), 8), :] = n[8 * kt : 8 * kt + 8]
            return c

        lax.fori_loop(first, first + count, step, 0, unroll=2)

    for k in range(MATS):
        packed[k] = flat[pl.ds((k // 8) * 704 + k % 8, T, stride=8), :].astype(jnp.bfloat16)

    planned.wait()
    pl.semaphore_wait(barrier, 14)

    def announce(s, c):
        there = 8 * ((row + s) % 8) + col
        pl.semaphore_signal(met_sem, inc=1, device_id={"dp": there}, device_id_type=MESH)
        return c

    lax.fori_loop(1, 8, announce, 0, unroll=True)

    def deliver(p):
        send[p] = packed[table[0, 0, p]]

        @pl.when(p == me)
        def _():
            pltpu.make_async_copy(send.at[p], held.at[p], recv_sem).start()

        @pl.when(p != me)
        def _():
            pltpu.make_async_remote_copy(
                send.at[p], held.at[me], send_sem, recv_sem, device_id={"dp": p}, device_id_type=MESH
            ).start()

    def to_column(s, c):
        deliver(8 * ((row + ring_offset(s)) % 8) + col)
        return c

    lax.fori_loop(0, 7, to_column, 0)
    pl.semaphore_wait(met_sem, 7)

    def deliver_outside(p):
        @pl.when((p % 8 != col) | (p == me))
        def _():
            deliver(p)

    def to_fixed(s, c):
        there = (row + ring_offset(s % 8)) % 8
        deliver_outside(fixed_device(3 * there + (s // 8 + col) % 3))
        return c

    lax.fori_loop(0, FIXED, to_fixed, 0)

    def to_rest(s, c):
        there = (row + ring_offset(s % 8)) % 8
        deliver_outside(other_device(there, (s // 8 + col) % 5))
        return c

    lax.fori_loop(0, N - FIXED, to_rest, 0)

    def find(k, c):
        where = jnp.int32(0)
        for d in range(FIXED):
            where = jnp.where(table[0, 0, fixed_device(d)] == k, d, where)
        place[k] = where
        return c

    lax.fori_loop(0, MATS, find, 0)

    pltpu.make_async_copy(held, held, recv_sem).wait()

    def unpack(q, total):
        block = held[q].astype(jnp.float32)
        flat[pl.ds(pl.multiple_of(q * T, 8), T), :] = block
        return total + jnp.sum((block * block).reshape(T // 8, 8, 128), axis=0)

    total = lax.fori_loop(0, N, unpack, jnp.zeros((8, 128), jnp.float32), unroll=2)
    inverse = 1.0 / (jnp.sqrt(jnp.sum(total)) + EPSILON)

    def normalize(i, c):
        rows = pl.ds(pl.multiple_of(i * 64, 64), 64)
        for t in range(TILES):
            part = flat[pl.ds(i * 512 + t, 64, stride=8), :]
            x[rows, 128 * t : 128 * t + 128] = (part * inverse).astype(jnp.bfloat16)
        return c

    lax.fori_loop(0, R // 64, normalize, 0)
    x[R:, :] = jnp.zeros((RP - R, C), jnp.bfloat16)

    def polynomial(source):
        @pl.loop(0, 3)
        def _(i):
            rows = pl.ds(pl.multiple_of(i * 256, 256), 256)
            gram[rows, :] = lax.dot_general(
                source[rows, :], source[...], NT, preferred_element_type=jnp.float32
            ).astype(jnp.bfloat16)

        @pl.loop(0, 3)
        def _(i):
            rows = pl.ds(pl.multiple_of(i * 256, 256), 256)
            here = gram[rows, :]
            square = jnp.dot(here, gram[...], preferred_element_type=jnp.float32)
            poly[rows, :] = (COEF_B * here.astype(jnp.float32) + COEF_C * square).astype(jnp.bfloat16)

    polynomial(x)

    @pl.loop(0, 3)
    def _(i):
        rows = pl.ds(pl.multiple_of(i * 256, 256), 256)
        y = COEF_A * x[rows, :].astype(jnp.float32) + jnp.dot(
            poly[rows, :], x[...], preferred_element_type=jnp.float32
        )
        x1[rows, :] = y.astype(jnp.bfloat16)

    polynomial(x1)
    owns = table[1, 0, me] > 0

    for t in range(TILES // 2):
        columns = slice(256 * t, 256 * t + 256)
        z = SCALE * (
            COEF_A * x1[:R, columns].astype(jnp.float32)
            + jnp.dot(poly[:R, :], x1[:, columns], preferred_element_type=jnp.float32)
        )
        z_owned = jnp.where(owns, z, 0.0).astype(jnp.bfloat16)
        for i, (first, count) in enumerate(ROWS):
            owned[i][:, columns] = z_owned[first : first + count]
        for h in range(2):
            flat[pl.ds(2 * t + h, R, stride=8), :] = z[:, 128 * h : 128 * h + 128]

    @pl.when(is_fixed)
    def _():
        def give(s, c):
            p = 8 * ((row + ring_offset(s % 8)) % 8) + (s // 8 + col) % 8
            back[p] = flat[pl.ds(pl.multiple_of(p * T, 8), T), :].astype(jnp.bfloat16)

            @pl.when(p == me)
            def _():
                pltpu.make_async_copy(back.at[p], got.at[mine], got_sem).start()

            @pl.when(p != me)
            def _():
                pltpu.make_async_remote_copy(
                    back.at[p], got.at[mine], back_sem, got_sem, device_id={"dp": p}, device_id_type=MESH
                ).start()

            return c

        lax.fori_loop(0, N, give, 0)

    sent = send.at[pl.ds(0, N - 1)]
    pltpu.make_async_copy(sent, sent, send_sem).wait()
    pltpu.make_async_copy(got, got, got_sem).wait()

    for k in range(MATS):
        flat[pl.ds((k // 8) * 704 + k % 8, T, stride=8), :] = got[place[k]].astype(jnp.float32)

    for i, (first, count) in enumerate(PARTS):

        def write(t, c):
            columns = pl.ds(pl.multiple_of((t - first) * 128, 128), 128)
            parts = [flat[pl.ds(pl.multiple_of(kt * 704 + t * 8, 8), 8), :] for kt in range(3)]
            update[i][:, columns] = jnp.concatenate(parts, axis=0).astype(jnp.bfloat16)
            return c

        lax.fori_loop(first, first + count, write, 0, unroll=2)

    @pl.when(is_fixed)
    def _():
        gone = back.at[pl.ds(0, N - 1)]
        pltpu.make_async_copy(gone, gone, back_sem).wait()


def write_kernel(*refs):
    pieces, (new_momentum, update, owned), sems = refs[:9], refs[9:12], refs[12]
    copies = []
    for i in range(3):
        columns = pl.ds(128 * PARTS[i][0], 128 * PARTS[i][1])
        copies += [
            pltpu.make_async_copy(pieces[6 + i], owned.at[0, pl.ds(*ROWS[i]), :], sems.at[6 + i]),
            pltpu.make_async_copy(pieces[i], new_momentum.at[:, columns], sems.at[i]),
            pltpu.make_async_copy(pieces[3 + i], update.at[:, columns], sems.at[3 + i]),
        ]
    for copy in copies:
        copy.start()
    for copy in copies:
        copy.wait()


def body(grad, momentum, owners):
    hbm = pl.BlockSpec(memory_space=pltpu.HBM)
    vmem = pl.BlockSpec(memory_space=pltpu.VMEM)
    bf16, f32, i32 = jnp.bfloat16, jnp.float32, jnp.int32
    pieces = (
        *(jax.ShapeDtypeStruct((MATS, 128 * count), f32) for _, count in PARTS),
        *(jax.ShapeDtypeStruct((MATS, 128 * count), bf16) for _, count in PARTS),
        *(jax.ShapeDtypeStruct((count, C), bf16) for _, count in ROWS),
    )
    results = pl.pallas_call(
        kernel,
        out_shape=pieces,
        in_specs=[hbm, hbm, hbm],
        out_specs=(vmem,) * 9,
        scratch_shapes=[
            pltpu.SMEM((MATS,), i32),
            pltpu.VMEM(grad.shape, bf16),
            pltpu.VMEM(momentum.shape, f32),
            pltpu.VMEM((2, 8, 128), i32),
            pltpu.VMEM((MATS, T, 128), bf16),
            pltpu.SMEM((2, 8, 128), i32),
            pltpu.SMEM((MATS,), i32),
            pltpu.VMEM((N * T, 128), f32),
            pltpu.VMEM((N, T, 128), bf16),
            pltpu.VMEM((N, T, 128), bf16),
            pltpu.VMEM((RP, C), bf16),
            pltpu.VMEM((RP, C), bf16),
            pltpu.VMEM((RP, RP), bf16),
            pltpu.VMEM((RP, RP), bf16),
            pltpu.VMEM((N, T, 128), bf16),
            pltpu.VMEM((FIXED, T, 128), bf16),
            pltpu.SemaphoreType.DMA((2 * len(PARTS) + 1,)),
            pltpu.SemaphoreType.REGULAR,
            pltpu.SemaphoreType.DMA,
            pltpu.SemaphoreType.DMA,
            pltpu.SemaphoreType.DMA,
            pltpu.SemaphoreType.DMA,
        ],
        compiler_params=pltpu.CompilerParams(
            collective_id=0, has_side_effects=True, vmem_limit_bytes=MAIN_KIB << 10
        ),
    )(owners, grad, momentum)
    return pl.pallas_call(
        write_kernel,
        out_shape=(
            jax.ShapeDtypeStruct(momentum.shape, f32),
            jax.ShapeDtypeStruct(grad.shape, bf16),
            jax.ShapeDtypeStruct((1, R, C), bf16),
        ),
        in_specs=[vmem] * 9,
        out_specs=(hbm, hbm, hbm),
        scratch_shapes=[pltpu.SemaphoreType.DMA((9,))],
        compiler_params=pltpu.CompilerParams(vmem_limit_bytes=4 << 20),
    )(*results)


def solution(mesh):
    return jax.shard_map(
        body,
        mesh=mesh,
        in_specs=(P("rep", "dp"), P("rep", "dp"), P("rep")),
        out_specs=(P("rep", "dp"), P("rep", "dp"), P(("rep", "dp"), None, None)),
        check_vma=False,
    )
```

```python
import math

import jax
import jax.numpy as jnp
from jax import lax
from jax.experimental import pallas as pl
from jax.experimental.pallas import tpu as pltpu
from jax.sharding import PartitionSpec as P

R = 704
C = 1024
RP = 768
MATS = 24
N = 64
T = 88
TILES = C // 128
PARTS = ((0, 30), (30, 30), (60, 28))
ROWS = ((0, 240), (240, 240), (480, 224))
MAIN_KIB = 52000
AHEAD = 1
FIXED = 24

MOMENTUM_RATE = 0.95
EPSILON = 1e-07
COEF_A = 3.4445
COEF_B = -4.775
COEF_C = 2.0315
SCALE = 0.2 * math.sqrt(max(R, C))
MESH = pl.DeviceIdType.MESH
NT = (((1,), (1,)), ((), ()))


def ring_offset(u):
    v = 7 - u
    odd = v % 2
    return odd * ((v + 1) // 2) + (1 - odd) * (8 - v // 2)


def fixed_device(d):
    row = d // 3
    return 8 * row + (3 * (d % 3) + 6 * row) % 8


def other_device(row, i):
    return 8 * row + (i + 1 + i // 2 + 6 * row) % 8


def kernel(
    owners_hbm, grad_hbm, momentum_hbm,
    *refs,
):
    new_momentum, update, owned = refs[0:3], refs[3:6], refs[6:9]
    (
        owners, grad, momentum, plan, packed, table, place,
        flat, send, held, x, x1, gram, poly, back, got,
        load_sem, met_sem, send_sem, recv_sem, back_sem, got_sem,
    ) = refs[9:]
    me = lax.axis_index("dp")
    row, col = me // 8, me % 8
    turned = (col + 2 * row) % 8
    is_fixed = turned % 3 == 0
    mine = 3 * row + turned // 3

    def load(i):
        columns = pl.ds(128 * PARTS[i][0], 128 * PARTS[i][1])
        return (
            pltpu.make_async_copy(grad_hbm.at[:, columns], grad.at[:, columns], load_sem.at[2 * i]),
            pltpu.make_async_copy(momentum_hbm.at[:, columns], momentum.at[:, columns], load_sem.at[2 * i + 1]),
        )

    whose = pltpu.make_async_copy(owners_hbm, owners, load_sem.at[2 * len(PARTS)])
    planned = pltpu.make_async_copy(plan, table, load_sem.at[2 * len(PARTS)])
    whose.start()
    for i in range(len(PARTS)):
        for copy in load(i):
            copy.start()

    barrier = pltpu.get_barrier_semaphore()

    def greet(s, c):
        there = 8 * ((row + s) % 8) + col
        pl.semaphore_signal(barrier, inc=1, device_id={"dp": there}, device_id_type=MESH)
        there = 8 * row + (col + s) % 8
        pl.semaphore_signal(barrier, inc=1, device_id={"dp": there}, device_id_type=MESH)
        return c

    lax.fori_loop(1, 8, greet, 0, unroll=True)
    whose.wait()
    lane = lax.broadcasted_iota(jnp.int32, (8, 128), 1)
    matrix = jnp.zeros((8, 128), jnp.int32)
    owning = jnp.zeros((8, 128), jnp.int32)
    for k in range(MATS):
        here = lane == owners[k]
        matrix = jnp.where(here, k, matrix)
        owning = jnp.where(here, 1, owning)
    in_fixed = lambda c: (c == 0) | (c == 3) | (c == 6)
    free = in_fixed((lane + 2 * (lane // 8)) & 7) & (lane < N) & (owning == 0)
    rank = jnp.where(free, 1, 0)
    for shift in (1, 2, 4, 8, 16, 32):
        rank = rank + jnp.where(lane >= shift, pltpu.roll(rank, shift, 1), 0)
    rank = jnp.where(free, rank, 0)
    count = jnp.int32(0)
    for k in range(MATS):
        outside = jnp.where(in_fixed((owners[k] + 2 * (owners[k] // 8)) & 7), 0, 1)
        count = count + outside
        matrix = jnp.where(rank == count * outside + (outside - 1), k, matrix)
    plan[0] = matrix
    plan[1] = owning

    planned.start()

    for i, (first, count) in enumerate(PARTS):
        for copy in load(i):
            copy.wait()

        def step(t, c):
            columns = pl.ds(pl.multiple_of(t * 128, 128), 128)
            g = grad[:, columns].astype(jnp.float32)
            m = MOMENTUM_RATE * momentum[:, columns] + g
            new_momentum[i][:, pl.ds(pl.multiple_of((t - first) * 128, 128), 128)] = m
            n = (g + MOMENTUM_RATE * m).astype(jnp.bfloat16).astype(jnp.float32)
            for kt in range(3):
                flat[pl.ds(pl.multiple_of(kt * 704 + t * 8, 8), 8), :] = n[8 * kt : 8 * kt + 8]
            return c

        lax.fori_loop(first, first + count, step, 0, unroll=2)

    for k in range(MATS):
        packed[k] = flat[pl.ds((k // 8) * 704 + k % 8, T, stride=8), :].astype(jnp.bfloat16)

    planned.wait()
    pl.semaphore_wait(barrier, 14)

    def announce(s, c):
        there = 8 * ((row + s) % 8) + col
        pl.semaphore_signal(met_sem, inc=1, device_id={"dp": there}, device_id_type=MESH)
        return c

    lax.fori_loop(1, 8, announce, 0, unroll=True)

    def deliver(p):
        send[p] = packed[table[0, 0, p]]

        @pl.when(p == me)
        def _():
            pltpu.make_async_copy(send.at[p], held.at[p], recv_sem).start()

        @pl.when(p != me)
        def _():
            pltpu.make_async_remote_copy(
                send.at[p], held.at[me], send_sem, recv_sem, device_id={"dp": p}, device_id_type=MESH
            ).start()

    def to_column(s, c):
        deliver(8 * ((row + ring_offset(s)) % 8) + col)
        return c

    lax.fori_loop(0, 7, to_column, 0)
    pl.semaphore_wait(met_sem, 7)

    def deliver_outside(p):
        @pl.when((p % 8 != col) | (p == me))
        def _():
            deliver(p)

    def to_fixed(s, c):
        there = (row + ring_offset(s % 8)) % 8
        deliver_outside(fixed_device(3 * there + (s // 8 + col) % 3))
        return c

    lax.fori_loop(0, FIXED, to_fixed, 0)

    def to_rest(s, c):
        there = (row + ring_offset(s % 8)) % 8
        deliver_outside(other_device(there, (s // 8 + col) % 5))
        return c

    lax.fori_loop(0, N - FIXED, to_rest, 0)

    def find(k, c):
        where = jnp.int32(0)
        for d in range(FIXED):
            where = jnp.where(table[0, 0, fixed_device(d)] == k, d, where)
        place[k] = where
        return c

    lax.fori_loop(0, MATS, find, 0)

    pltpu.make_async_copy(held, held, recv_sem).wait()

    def unpack(q, total):
        block = held[q].astype(jnp.float32)
        flat[pl.ds(pl.multiple_of(q * T, 8), T), :] = block
        return total + jnp.sum((block * block).reshape(T // 8, 8, 128), axis=0)

    total = lax.fori_loop(0, N, unpack, jnp.zeros((8, 128), jnp.float32), unroll=2)
    inverse = 1.0 / (jnp.sqrt(jnp.sum(total)) + EPSILON)

    def normalize(i, c):
        rows = pl.ds(pl.multiple_of(i * 64, 64), 64)
        for t in range(TILES):
            part = flat[pl.ds(i * 512 + t, 64, stride=8), :]
            x[rows, 128 * t : 128 * t + 128] = (part * inverse).astype(jnp.bfloat16)
        return c

    lax.fori_loop(0, R // 64, normalize, 0)
    x[R:, :] = jnp.zeros((RP - R, C), jnp.bfloat16)

    def polynomial(source):
        @pl.loop(0, 3)
        def _(i):
            rows = pl.ds(pl.multiple_of(i * 256, 256), 256)
            gram[rows, :] = lax.dot_general(
                source[rows, :], source[...], NT, preferred_element_type=jnp.float32
            ).astype(jnp.bfloat16)

        @pl.loop(0, 3)
        def _(i):
            rows = pl.ds(pl.multiple_of(i * 256, 256), 256)
            here = gram[rows, :]
            square = jnp.dot(here, gram[...], preferred_element_type=jnp.float32)
            poly[rows, :] = (COEF_B * here.astype(jnp.float32) + COEF_C * square).astype(jnp.bfloat16)

    polynomial(x)

    @pl.loop(0, 3)
    def _(i):
        rows = pl.ds(pl.multiple_of(i * 256, 256), 256)
        y = COEF_A * x[rows, :].astype(jnp.float32) + jnp.dot(
            poly[rows, :], x[...], preferred_element_type=jnp.float32
        )
        x1[rows, :] = y.astype(jnp.bfloat16)

    polynomial(x1)
    owns = table[1, 0, me] > 0

    for t in range(TILES // 2):
        columns = slice(256 * t, 256 * t + 256)
        z = SCALE * (
            COEF_A * x1[:R, columns].astype(jnp.float32)
            + jnp.dot(poly[:R, :], x1[:, columns], preferred_element_type=jnp.float32)
        )
        z_owned = jnp.where(owns, z, 0.0).astype(jnp.bfloat16)
        for i, (first, count) in enumerate(ROWS):
            owned[i][:, columns] = z_owned[first : first + count]
        for h in range(2):
            flat[pl.ds(2 * t + h, R, stride=8), :] = z[:, 128 * h : 128 * h + 128]

    @pl.when(is_fixed)
    def _():
        def give(there, v):
            p = 8 * there + (v + col) % 8
            back[p] = flat[pl.ds(pl.multiple_of(p * T, 8), T), :].astype(jnp.bfloat16)

            @pl.when(p == me)
            def _():
                pltpu.make_async_copy(back.at[p], got.at[mine], got_sem).start()

            @pl.when(p != me)
            def _():
                pltpu.make_async_remote_copy(
                    back.at[p], got.at[mine], back_sem, got_sem, device_id={"dp": p}, device_id_type=MESH
                ).start()

        def to_early(s, c):
            give((s + row) % 4, s // 4)
            return c

        def to_both(s, c):
            there = (row + ring_offset(s % 8)) % 8
            early = 1 - there // 4
            give(there, s // 8 + AHEAD * early)
            return c

        def to_late(s, c):
            give(4 + (s + row) % 4, 8 - AHEAD + s // 4)
            return c

        lax.fori_loop(0, 4 * AHEAD, to_early, 0)
        lax.fori_loop(0, 8 * (8 - AHEAD), to_both, 0)
        lax.fori_loop(0, 4 * AHEAD, to_late, 0)

    sent = send.at[pl.ds(0, N - 1)]
    pltpu.make_async_copy(sent, sent, send_sem).wait()
    pltpu.make_async_copy(got, got, got_sem).wait()

    for k in range(MATS):
        flat[pl.ds((k // 8) * 704 + k % 8, T, stride=8), :] = got[place[k]].astype(jnp.float32)

    for i, (first, count) in enumerate(PARTS):

        def write(t, c):
            columns = pl.ds(pl.multiple_of((t - first) * 128, 128), 128)
            parts = [flat[pl.ds(pl.multiple_of(kt * 704 + t * 8, 8), 8), :] for kt in range(3)]
            update[i][:, columns] = jnp.concatenate(parts, axis=0).astype(jnp.bfloat16)
            return c

        lax.fori_loop(first, first + count, write, 0, unroll=2)

    @pl.when(is_fixed)
    def _():
        gone = back.at[pl.ds(0, N - 1)]
        pltpu.make_async_copy(gone, gone, back_sem).wait()


def write_kernel(*refs):
    pieces, (new_momentum, update, owned), sems = refs[:9], refs[9:12], refs[12]
    copies = []
    for i in range(3):
        columns = pl.ds(128 * PARTS[i][0], 128 * PARTS[i][1])
        copies += [
            pltpu.make_async_copy(pieces[6 + i], owned.at[0, pl.ds(*ROWS[i]), :], sems.at[6 + i]),
            pltpu.make_async_copy(pieces[i], new_momentum.at[:, columns], sems.at[i]),
            pltpu.make_async_copy(pieces[3 + i], update.at[:, columns], sems.at[3 + i]),
        ]
    for copy in copies:
        copy.start()
    for copy in copies:
        copy.wait()


def body(grad, momentum, owners):
    hbm = pl.BlockSpec(memory_space=pltpu.HBM)
    vmem = pl.BlockSpec(memory_space=pltpu.VMEM)
    bf16, f32, i32 = jnp.bfloat16, jnp.float32, jnp.int32
    pieces = (
        *(jax.ShapeDtypeStruct((MATS, 128 * count), f32) for _, count in PARTS),
        *(jax.ShapeDtypeStruct((MATS, 128 * count), bf16) for _, count in PARTS),
        *(jax.ShapeDtypeStruct((count, C), bf16) for _, count in ROWS),
    )
    results = pl.pallas_call(
        kernel,
        out_shape=pieces,
        in_specs=[hbm, hbm, hbm],
        out_specs=(vmem,) * 9,
        scratch_shapes=[
            pltpu.SMEM((MATS,), i32),
            pltpu.VMEM(grad.shape, bf16),
            pltpu.VMEM(momentum.shape, f32),
            pltpu.VMEM((2, 8, 128), i32),
            pltpu.VMEM((MATS, T, 128), bf16),
            pltpu.SMEM((2, 8, 128), i32),
            pltpu.SMEM((MATS,), i32),
            pltpu.VMEM((N * T, 128), f32),
            pltpu.VMEM((N, T, 128), bf16),
            pltpu.VMEM((N, T, 128), bf16),
            pltpu.VMEM((RP, C), bf16),
            pltpu.VMEM((RP, C), bf16),
            pltpu.VMEM((RP, RP), bf16),
            pltpu.VMEM((RP, RP), bf16),
            pltpu.VMEM((N, T, 128), bf16),
            pltpu.VMEM((FIXED, T, 128), bf16),
            pltpu.SemaphoreType.DMA((2 * len(PARTS) + 1,)),
            pltpu.SemaphoreType.REGULAR,
            pltpu.SemaphoreType.DMA,
            pltpu.SemaphoreType.DMA,
            pltpu.SemaphoreType.DMA,
            pltpu.SemaphoreType.DMA,
        ],
        compiler_params=pltpu.CompilerParams(
            collective_id=0, has_side_effects=True, vmem_limit_bytes=MAIN_KIB << 10
        ),
    )(owners, grad, momentum)
    return pl.pallas_call(
        write_kernel,
        out_shape=(
            jax.ShapeDtypeStruct(momentum.shape, f32),
            jax.ShapeDtypeStruct(grad.shape, bf16),
            jax.ShapeDtypeStruct((1, R, C), bf16),
        ),
        in_specs=[vmem] * 9,
        out_specs=(hbm, hbm, hbm),
        scratch_shapes=[pltpu.SemaphoreType.DMA((9,))],
        compiler_params=pltpu.CompilerParams(vmem_limit_bytes=4 << 20),
    )(*results)


def solution(mesh):
    return jax.shard_map(
        body,
        mesh=mesh,
        in_specs=(P("rep", "dp"), P("rep", "dp"), P("rep")),
        out_specs=(P("rep", "dp"), P("rep", "dp"), P(("rep", "dp"), None, None)),
        check_vma=False,
    )
```

```python
import math

import jax
import jax.numpy as jnp
from jax import lax
from jax.experimental import pallas as pl
from jax.experimental.pallas import tpu as pltpu
from jax.sharding import PartitionSpec as P

R = 704
C = 1024
RP = 768
MATS = 24
N = 64
T = 88
TILES = C // 128
PARTS = ((0, 30), (30, 30), (60, 28))
ROWS = ((0, 240), (240, 240), (480, 224))
MAIN_KIB = 52000
AHEAD = 1
FIXED = 24

MOMENTUM_RATE = 0.95
EPSILON = 1e-07
COEF_A = 3.4445
COEF_B = -4.775
COEF_C = 2.0315
SCALE = 0.2 * math.sqrt(max(R, C))
MESH = pl.DeviceIdType.MESH
NT = (((1,), (1,)), ((), ()))


def ring_offset(u):
    v = 7 - u
    odd = v % 2
    return odd * ((v + 1) // 2) + (1 - odd) * (8 - v // 2)


def fixed_device(d):
    row = d // 3
    return 8 * row + (3 * (d % 3) + 6 * row) % 8


def other_device(row, i):
    return 8 * row + (i + 1 + i // 2 + 6 * row) % 8


def kernel(
    owners_hbm, grad_hbm, momentum_hbm,
    *refs,
):
    new_momentum, update, owned = refs[0:3], refs[3:6], refs[6:9]
    (
        owners, grad, momentum, plan, packed, table, place,
        flat, send, held, x, x1, gram, poly, back, got,
        load_sem, met_sem, send_sem, recv_sem, back_sem, got_sem,
    ) = refs[9:]
    me = lax.axis_index("dp")
    row, col = me // 8, me % 8
    turned = (col + 2 * row) % 8
    is_fixed = turned % 3 == 0
    mine = 3 * row + turned // 3

    def load(i):
        columns = pl.ds(128 * PARTS[i][0], 128 * PARTS[i][1])
        return (
            pltpu.make_async_copy(grad_hbm.at[:, columns], grad.at[:, columns], load_sem.at[2 * i]),
            pltpu.make_async_copy(momentum_hbm.at[:, columns], momentum.at[:, columns], load_sem.at[2 * i + 1]),
        )

    whose = pltpu.make_async_copy(owners_hbm, owners, load_sem.at[2 * len(PARTS)])
    planned = pltpu.make_async_copy(plan, table, load_sem.at[2 * len(PARTS)])
    whose.start()
    for i in range(len(PARTS)):
        for copy in load(i):
            copy.start()

    barrier = pltpu.get_barrier_semaphore()

    def greet(s, c):
        there = 8 * ((row + s) % 8) + col
        pl.semaphore_signal(barrier, inc=1, device_id={"dp": there}, device_id_type=MESH)
        there = 8 * row + (col + s) % 8
        pl.semaphore_signal(barrier, inc=1, device_id={"dp": there}, device_id_type=MESH)
        return c

    lax.fori_loop(1, 8, greet, 0, unroll=True)
    whose.wait()
    lane = lax.broadcasted_iota(jnp.int32, (8, 128), 1)
    matrix = jnp.zeros((8, 128), jnp.int32)
    owning = jnp.zeros((8, 128), jnp.int32)
    for k in range(MATS):
        here = lane == owners[k]
        matrix = jnp.where(here, k, matrix)
        owning = jnp.where(here, 1, owning)
    in_fixed = lambda c: (c == 0) | (c == 3) | (c == 6)
    free = in_fixed((lane + 2 * (lane // 8)) & 7) & (lane < N) & (owning == 0)
    rank = jnp.where(free, 1, 0)
    for shift in (1, 2, 4, 8, 16, 32):
        rank = rank + jnp.where(lane >= shift, pltpu.roll(rank, shift, 1), 0)
    rank = jnp.where(free, rank, 0)
    count = jnp.int32(0)
    for k in range(MATS):
        outside = jnp.where(in_fixed((owners[k] + 2 * (owners[k] // 8)) & 7), 0, 1)
        count = count + outside
        matrix = jnp.where(rank == count * outside + (outside - 1), k, matrix)
    plan[0] = matrix
    plan[1] = owning

    planned.start()

    for i, (first, count) in enumerate(PARTS):
        for copy in load(i):
            copy.wait()

        def step(t, c):
            columns = pl.ds(pl.multiple_of(t * 128, 128), 128)
            g = grad[:, columns].astype(jnp.float32)
            m = MOMENTUM_RATE * momentum[:, columns] + g
            new_momentum[i][:, pl.ds(pl.multiple_of((t - first) * 128, 128), 128)] = m
            n = (g + MOMENTUM_RATE * m).astype(jnp.bfloat16).astype(jnp.float32)
            for kt in range(3):
                flat[pl.ds(pl.multiple_of(kt * 704 + t * 8, 8), 8), :] = n[8 * kt : 8 * kt + 8]
            return c

        lax.fori_loop(first, first + count, step, 0, unroll=2)

    for k in range(MATS):
        packed[k] = flat[pl.ds((k // 8) * 704 + k % 8, T, stride=8), :].astype(jnp.bfloat16)

    planned.wait()
    pl.semaphore_wait(barrier, 14)

    def announce(s, c):
        there = 8 * ((row + s) % 8) + col
        pl.semaphore_signal(met_sem, inc=1, device_id={"dp": there}, device_id_type=MESH)
        return c

    lax.fori_loop(1, 8, announce, 0, unroll=True)

    def deliver(p):
        send[p] = packed[table[0, 0, p]]

        @pl.when(p == me)
        def _():
            pltpu.make_async_copy(send.at[p], held.at[p], recv_sem).start()

        @pl.when(p != me)
        def _():
            pltpu.make_async_remote_copy(
                send.at[p], held.at[me], send_sem, recv_sem, device_id={"dp": p}, device_id_type=MESH
            ).start()

    def to_column(s, c):
        deliver(8 * ((row + ring_offset(s)) % 8) + col)
        return c

    lax.fori_loop(0, 7, to_column, 0)
    pl.semaphore_wait(met_sem, 7)

    def deliver_outside(p):
        @pl.when((p % 8 != col) | (p == me))
        def _():
            deliver(p)

    def to_fixed(s, c):
        there = (row + ring_offset(s % 8)) % 8
        deliver_outside(fixed_device(3 * there + (s // 8 + col) % 3))
        return c

    lax.fori_loop(0, FIXED, to_fixed, 0)

    def to_rest(s, c):
        there = (row + ring_offset(s % 8)) % 8
        deliver_outside(other_device(there, (s // 8 + col) % 5))
        return c

    lax.fori_loop(0, N - FIXED, to_rest, 0)

    def find(k, c):
        where = jnp.int32(0)
        for d in range(FIXED):
            where = jnp.where(table[0, 0, fixed_device(d)] == k, d, where)
        place[k] = where
        return c

    lax.fori_loop(0, MATS, find, 0)

    pltpu.make_async_copy(held, held, recv_sem).wait()

    def unpack(q, total):
        block = held[q].astype(jnp.float32)
        flat[pl.ds(pl.multiple_of(q * T, 8), T), :] = block
        return total + jnp.sum((block * block).reshape(T // 8, 8, 128), axis=0)

    total = lax.fori_loop(0, N, unpack, jnp.zeros((8, 128), jnp.float32), unroll=2)
    inverse = 1.0 / (jnp.sqrt(jnp.sum(total)) + EPSILON)

    def normalize(i, c):
        rows = pl.ds(pl.multiple_of(i * 64, 64), 64)
        for t in range(TILES):
            part = flat[pl.ds(i * 512 + t, 64, stride=8), :]
            x[rows, 128 * t : 128 * t + 128] = (part * inverse).astype(jnp.bfloat16)
        return c

    lax.fori_loop(0, R // 64, normalize, 0)
    x[R:, :] = jnp.zeros((RP - R, C), jnp.bfloat16)

    def polynomial(source):
        @pl.loop(0, 3)
        def _(i):
            rows = pl.ds(pl.multiple_of(i * 256, 256), 256)
            gram[rows, :] = lax.dot_general(
                source[rows, :], source[...], NT, preferred_element_type=jnp.float32
            ).astype(jnp.bfloat16)

        @pl.loop(0, 3)
        def _(i):
            rows = pl.ds(pl.multiple_of(i * 256, 256), 256)
            here = gram[rows, :]
            square = jnp.dot(here, gram[...], preferred_element_type=jnp.float32)
            poly[rows, :] = (COEF_B * here.astype(jnp.float32) + COEF_C * square).astype(jnp.bfloat16)

    polynomial(x)

    @pl.loop(0, 3)
    def _(i):
        rows = pl.ds(pl.multiple_of(i * 256, 256), 256)
        y = COEF_A * x[rows, :].astype(jnp.float32) + jnp.dot(
            poly[rows, :], x[...], preferred_element_type=jnp.float32
        )
        x1[rows, :] = y.astype(jnp.bfloat16)

    polynomial(x1)
    owns = table[1, 0, me] > 0

    for t in range(TILES // 2):
        columns = slice(256 * t, 256 * t + 256)
        z = SCALE * (
            COEF_A * x1[:R, columns].astype(jnp.float32)
            + jnp.dot(poly[:R, :], x1[:, columns], preferred_element_type=jnp.float32)
        )
        z_owned = jnp.where(owns, z, 0.0).astype(jnp.bfloat16)
        for i, (first, count) in enumerate(ROWS):
            owned[i][:, columns] = z_owned[first : first + count]
        for h in range(2):
            flat[pl.ds(2 * t + h, R, stride=8), :] = z[:, 128 * h : 128 * h + 128]

    @pl.when(is_fixed)
    def _():
        def give(there, v):
            p = 8 * there + (v + col) % 8
            back[p] = flat[pl.ds(pl.multiple_of(p * T, 8), T), :].astype(jnp.bfloat16)

            @pl.when(p == me)
            def _():
                pltpu.make_async_copy(back.at[p], got.at[mine], got_sem).start()

            @pl.when(p != me)
            def _():
                pltpu.make_async_remote_copy(
                    back.at[p], got.at[mine], back_sem, got_sem, device_id={"dp": p}, device_id_type=MESH
                ).start()

        def to_early(s, c):
            give((s + row) % 4, s // 4)
            return c

        def to_both(s, c):
            there = (row + ring_offset(s % 8)) % 8
            early = 1 - there // 4
            give(there, s // 8 + AHEAD * early)
            return c

        def to_late(s, c):
            give(4 + (s + row) % 4, 8 - AHEAD + s // 4)
            return c

        lax.fori_loop(0, 4 * AHEAD, to_early, 0)
        lax.fori_loop(0, 8 * (8 - AHEAD), to_both, 0)
        lax.fori_loop(0, 4 * AHEAD, to_late, 0)

    sent = send.at[pl.ds(0, N - 1)]
    pltpu.make_async_copy(sent, sent, send_sem).wait()
    pltpu.make_async_copy(got, got, got_sem).wait()

    for k in range(MATS):
        flat[pl.ds((k // 8) * 704 + k % 8, T, stride=8), :] = got[place[k]].astype(jnp.float32)

    for i, (first, count) in enumerate(PARTS):

        def write(t, c):
            columns = pl.ds(pl.multiple_of((t - first) * 128, 128), 128)
            parts = [flat[pl.ds(pl.multiple_of(kt * 704 + t * 8, 8), 8), :] for kt in range(3)]
            update[i][:, columns] = jnp.concatenate(parts, axis=0).astype(jnp.bfloat16)
            return c

        lax.fori_loop(first, first + count, write, 0, unroll=2)

    @pl.when(is_fixed)
    def _():
        gone = back.at[pl.ds(0, N - 1)]
        pltpu.make_async_copy(gone, gone, back_sem).wait()


def write_kernel(*refs):
    pieces, (new_momentum, update, owned), sems = refs[:9], refs[9:12], refs[12]
    copies = []
    for i in range(3):
        columns = pl.ds(128 * PARTS[i][0], 128 * PARTS[i][1])
        copies += [
            pltpu.make_async_copy(pieces[6 + i], owned.at[0, pl.ds(*ROWS[i]), :], sems.at[6 + i]),
            pltpu.make_async_copy(pieces[i], new_momentum.at[:, columns], sems.at[i]),
            pltpu.make_async_copy(pieces[3 + i], update.at[:, columns], sems.at[3 + i]),
        ]
    for copy in copies:
        copy.start()
    for copy in copies:
        copy.wait()


def body(grad, momentum, owners):
    hbm = pl.BlockSpec(memory_space=pltpu.HBM)
    vmem = pl.BlockSpec(memory_space=pltpu.VMEM)
    bf16, f32, i32 = jnp.bfloat16, jnp.float32, jnp.int32
    pieces = (
        *(jax.ShapeDtypeStruct((MATS, 128 * count), f32) for _, count in PARTS),
        *(jax.ShapeDtypeStruct((MATS, 128 * count), bf16) for _, count in PARTS),
        *(jax.ShapeDtypeStruct((count, C), bf16) for _, count in ROWS),
    )
    results = pl.pallas_call(
        kernel,
        out_shape=pieces,
        in_specs=[hbm, hbm, hbm],
        out_specs=(vmem,) * 9,
        scratch_shapes=[
            pltpu.SMEM((MATS,), i32),
            pltpu.VMEM(grad.shape, bf16),
            pltpu.VMEM(momentum.shape, f32),
            pltpu.VMEM((2, 8, 128), i32),
            pltpu.VMEM((MATS, T, 128), bf16),
            pltpu.SMEM((2, 8, 128), i32),
            pltpu.SMEM((MATS,), i32),
            pltpu.VMEM((N * T + 8, 128), f32),
            pltpu.VMEM((N, T, 128), bf16),
            pltpu.VMEM((N, T, 128), bf16),
            pltpu.VMEM((RP, C), bf16),
            pltpu.VMEM((RP, C), bf16),
            pltpu.VMEM((RP, RP), bf16),
            pltpu.VMEM((RP, RP), bf16),
            pltpu.VMEM((N, T, 128), bf16),
            pltpu.VMEM((FIXED, T, 128), bf16),
            pltpu.SemaphoreType.DMA((2 * len(PARTS) + 1,)),
            pltpu.SemaphoreType.REGULAR,
            pltpu.SemaphoreType.DMA,
            pltpu.SemaphoreType.DMA,
            pltpu.SemaphoreType.DMA,
            pltpu.SemaphoreType.DMA,
        ],
        compiler_params=pltpu.CompilerParams(
            collective_id=0, has_side_effects=True, vmem_limit_bytes=MAIN_KIB << 10
        ),
    )(owners, grad, momentum)
    return pl.pallas_call(
        write_kernel,
        out_shape=(
            jax.ShapeDtypeStruct(momentum.shape, f32),
            jax.ShapeDtypeStruct(grad.shape, bf16),
            jax.ShapeDtypeStruct((1, R, C), bf16),
        ),
        in_specs=[vmem] * 9,
        out_specs=(hbm, hbm, hbm),
        scratch_shapes=[pltpu.SemaphoreType.DMA((9,))],
        compiler_params=pltpu.CompilerParams(vmem_limit_bytes=4 << 20),
    )(*results)


def solution(mesh):
    return jax.shard_map(
        body,
        mesh=mesh,
        in_specs=(P("rep", "dp"), P("rep", "dp"), P("rep")),
        out_specs=(P("rep", "dp"), P("rep", "dp"), P(("rep", "dp"), None, None)),
        check_vma=False,
    )
```

```python
import math

import jax
import jax.numpy as jnp
from jax import lax
from jax.experimental import pallas as pl
from jax.experimental.pallas import tpu as pltpu
from jax.sharding import PartitionSpec as P

R = 704
C = 1024
RP = 768
MATS = 24
N = 64
T = 88
TILES = C // 128
PARTS = ((0, 30), (30, 30), (60, 28))
ROWS = ((0, 240), (240, 240), (480, 224))
MAIN_KIB = 52000
AHEAD = 1
FIXED = 24

MOMENTUM_RATE = 0.95
EPSILON = 1e-07
COEF_A = 3.4445
COEF_B = -4.775
COEF_C = 2.0315
SCALE = 0.2 * math.sqrt(max(R, C))
MESH = pl.DeviceIdType.MESH
NT = (((1,), (1,)), ((), ()))


def ring_offset(u):
    v = 7 - u
    odd = v % 2
    return odd * ((v + 1) // 2) + (1 - odd) * (8 - v // 2)


def fixed_device(d):
    row = d // 3
    return 8 * row + (3 * (d % 3) + 6 * row) % 8


def other_device(row, i):
    return 8 * row + (i + 1 + i // 2 + 6 * row) % 8


def kernel(
    owners_hbm, grad_hbm, momentum_hbm,
    *refs,
):
    new_momentum, update, owned = refs[0:3], refs[3:6], refs[6:9]
    (
        owners, grad, momentum, plan, packed, table, place,
        flat, send, held, x, x1, gram, poly, back, got,
        load_sem, met_sem, send_sem, recv_sem, back_sem, got_sem,
    ) = refs[9:]
    me = lax.axis_index("dp")
    row, col = me // 8, me % 8
    turned = (col + 2 * row) % 8
    is_fixed = turned % 3 == 0
    mine = 3 * row + turned // 3

    def load(i):
        columns = pl.ds(128 * PARTS[i][0], 128 * PARTS[i][1])
        return (
            pltpu.make_async_copy(grad_hbm.at[:, columns], grad.at[:, columns], load_sem.at[2 * i]),
            pltpu.make_async_copy(momentum_hbm.at[:, columns], momentum.at[:, columns], load_sem.at[2 * i + 1]),
        )

    whose = pltpu.make_async_copy(owners_hbm, owners, load_sem.at[2 * len(PARTS)])
    planned = pltpu.make_async_copy(plan, table, load_sem.at[2 * len(PARTS)])
    whose.start()
    for i in range(len(PARTS)):
        for copy in load(i):
            copy.start()

    barrier = pltpu.get_barrier_semaphore()

    def greet(s, c):
        there = 8 * ((row + s) % 8) + col
        pl.semaphore_signal(barrier, inc=1, device_id={"dp": there}, device_id_type=MESH)
        there = 8 * row + (col + s) % 8
        pl.semaphore_signal(barrier, inc=1, device_id={"dp": there}, device_id_type=MESH)
        return c

    lax.fori_loop(1, 8, greet, 0, unroll=True)
    whose.wait()
    lane = lax.broadcasted_iota(jnp.int32, (8, 128), 1)
    matrix = jnp.zeros((8, 128), jnp.int32)
    owning = jnp.zeros((8, 128), jnp.int32)
    for k in range(MATS):
        here = lane == owners[k]
        matrix = jnp.where(here, k, matrix)
        owning = jnp.where(here, 1, owning)
    in_fixed = lambda c: (c == 0) | (c == 3) | (c == 6)
    free = in_fixed((lane + 2 * (lane // 8)) & 7) & (lane < N) & (owning == 0)
    rank = jnp.where(free, 1, 0)
    for shift in (1, 2, 4, 8, 16, 32):
        rank = rank + jnp.where(lane >= shift, pltpu.roll(rank, shift, 1), 0)
    rank = jnp.where(free, rank, 0)
    count = jnp.int32(0)
    for k in range(MATS):
        outside = jnp.where(in_fixed((owners[k] + 2 * (owners[k] // 8)) & 7), 0, 1)
        count = count + outside
        matrix = jnp.where(rank == count * outside + (outside - 1), k, matrix)
    plan[0] = matrix
    plan[1] = owning

    planned.start()

    for i, (first, count) in enumerate(PARTS):
        for copy in load(i):
            copy.wait()

        def step(t, c):
            columns = pl.ds(pl.multiple_of(t * 128, 128), 128)
            g = grad[:, columns].astype(jnp.float32)
            m = MOMENTUM_RATE * momentum[:, columns] + g
            new_momentum[i][:, pl.ds(pl.multiple_of((t - first) * 128, 128), 128)] = m
            n = (g + MOMENTUM_RATE * m).astype(jnp.bfloat16).astype(jnp.float32)
            for kt in range(3):
                flat[pl.ds(pl.multiple_of(kt * 704 + t * 8, 8), 8), :] = n[8 * kt : 8 * kt + 8]
            return c

        lax.fori_loop(first, first + count, step, 0, unroll=2)

    pl.semaphore_wait(barrier, 14)

    def announce(s, c):
        there = 8 * ((row + s) % 8) + col
        pl.semaphore_signal(met_sem, inc=1, device_id={"dp": there}, device_id_type=MESH)
        return c

    lax.fori_loop(1, 8, announce, 0, unroll=True)

    for k in range(MATS):
        packed[k] = flat[pl.ds((k // 8) * 704 + k % 8, T, stride=8), :].astype(jnp.bfloat16)

    planned.wait()

    def deliver(p):
        send[p] = packed[table[0, 0, p]]

        @pl.when(p == me)
        def _():
            pltpu.make_async_copy(send.at[p], held.at[p], recv_sem).start()

        @pl.when(p != me)
        def _():
            pltpu.make_async_remote_copy(
                send.at[p], held.at[me], send_sem, recv_sem, device_id={"dp": p}, device_id_type=MESH
            ).start()

    def to_column(s, c):
        deliver(8 * ((row + ring_offset(s)) % 8) + col)
        return c

    lax.fori_loop(0, 7, to_column, 0)
    pl.semaphore_wait(met_sem, 7)

    def deliver_outside(p):
        @pl.when((p % 8 != col) | (p == me))
        def _():
            deliver(p)

    def to_fixed(s, c):
        there = (row + ring_offset(s % 8)) % 8
        deliver_outside(fixed_device(3 * there + (s // 8 + col) % 3))
        return c

    lax.fori_loop(0, FIXED, to_fixed, 0)

    def to_rest(s, c):
        there = (row + ring_offset(s % 8)) % 8
        deliver_outside(other_device(there, (s // 8 + col) % 5))
        return c

    lax.fori_loop(0, N - FIXED, to_rest, 0)

    def find(k, c):
        where = jnp.int32(0)
        for d in range(FIXED):
            where = jnp.where(table[0, 0, fixed_device(d)] == k, d, where)
        place[k] = where
        return c

    lax.fori_loop(0, MATS, find, 0)

    pltpu.make_async_copy(held, held, recv_sem).wait()

    def unpack(q, total):
        block = held[q].astype(jnp.float32)
        flat[pl.ds(pl.multiple_of(q * T, 8), T), :] = block
        return total + jnp.sum((block * block).reshape(T // 8, 8, 128), axis=0)

    total = lax.fori_loop(0, N, unpack, jnp.zeros((8, 128), jnp.float32), unroll=2)
    inverse = 1.0 / (jnp.sqrt(jnp.sum(total)) + EPSILON)

    def normalize(i, c):
        rows = pl.ds(pl.multiple_of(i * 64, 64), 64)
        for t in range(TILES):
            part = flat[pl.ds(i * 512 + t, 64, stride=8), :]
            x[rows, 128 * t : 128 * t + 128] = (part * inverse).astype(jnp.bfloat16)
        return c

    lax.fori_loop(0, R // 64, normalize, 0)
    x[R:, :] = jnp.zeros((RP - R, C), jnp.bfloat16)

    def polynomial(source):
        @pl.loop(0, 3)
        def _(i):
            rows = pl.ds(pl.multiple_of(i * 256, 256), 256)
            gram[rows, :] = lax.dot_general(
                source[rows, :], source[...], NT, preferred_element_type=jnp.float32
            ).astype(jnp.bfloat16)

        @pl.loop(0, 3)
        def _(i):
            rows = pl.ds(pl.multiple_of(i * 256, 256), 256)
            here = gram[rows, :]
            square = jnp.dot(here, gram[...], preferred_element_type=jnp.float32)
            poly[rows, :] = (COEF_B * here.astype(jnp.float32) + COEF_C * square).astype(jnp.bfloat16)

    polynomial(x)

    @pl.loop(0, 3)
    def _(i):
        rows = pl.ds(pl.multiple_of(i * 256, 256), 256)
        y = COEF_A * x[rows, :].astype(jnp.float32) + jnp.dot(
            poly[rows, :], x[...], preferred_element_type=jnp.float32
        )
        x1[rows, :] = y.astype(jnp.bfloat16)

    polynomial(x1)
    owns = table[1, 0, me] > 0

    for t in range(TILES // 2):
        columns = slice(256 * t, 256 * t + 256)
        z = SCALE * (
            COEF_A * x1[:R, columns].astype(jnp.float32)
            + jnp.dot(poly[:R, :], x1[:, columns], preferred_element_type=jnp.float32)
        )
        z_owned = jnp.where(owns, z, 0.0).astype(jnp.bfloat16)
        for i, (first, count) in enumerate(ROWS):
            owned[i][:, columns] = z_owned[first : first + count]
        for h in range(2):
            flat[pl.ds(2 * t + h, R, stride=8), :] = z[:, 128 * h : 128 * h + 128]

    @pl.when(is_fixed)
    def _():
        def give(there, v):
            p = 8 * there + (v + col) % 8
            back[p] = flat[pl.ds(pl.multiple_of(p * T, 8), T), :].astype(jnp.bfloat16)

            @pl.when(p == me)
            def _():
                pltpu.make_async_copy(back.at[p], got.at[mine], got_sem).start()

            @pl.when(p != me)
            def _():
                pltpu.make_async_remote_copy(
                    back.at[p], got.at[mine], back_sem, got_sem, device_id={"dp": p}, device_id_type=MESH
                ).start()

        def to_early(s, c):
            give((s + row) % 4, s // 4)
            return c

        def to_both(s, c):
            there = (row + ring_offset(s % 8)) % 8
            early = 1 - there // 4
            give(there, s // 8 + AHEAD * early)
            return c

        def to_late(s, c):
            give(4 + (s + row) % 4, 8 - AHEAD + s // 4)
            return c

        lax.fori_loop(0, 4 * AHEAD, to_early, 0)
        lax.fori_loop(0, 8 * (8 - AHEAD), to_both, 0)
        lax.fori_loop(0, 4 * AHEAD, to_late, 0)

    sent = send.at[pl.ds(0, N - 1)]
    pltpu.make_async_copy(sent, sent, send_sem).wait()
    pltpu.make_async_copy(got, got, got_sem).wait()

    for k in range(MATS):
        flat[pl.ds((k // 8) * 704 + k % 8, T, stride=8), :] = got[place[k]].astype(jnp.float32)

    for i, (first, count) in enumerate(PARTS):

        def write(t, c):
            columns = pl.ds(pl.multiple_of((t - first) * 128, 128), 128)
            parts = [flat[pl.ds(pl.multiple_of(kt * 704 + t * 8, 8), 8), :] for kt in range(3)]
            update[i][:, columns] = jnp.concatenate(parts, axis=0).astype(jnp.bfloat16)
            return c

        lax.fori_loop(first, first + count, write, 0, unroll=2)

    @pl.when(is_fixed)
    def _():
        gone = back.at[pl.ds(0, N - 1)]
        pltpu.make_async_copy(gone, gone, back_sem).wait()


def write_kernel(*refs):
    pieces, (new_momentum, update, owned), sems = refs[:9], refs[9:12], refs[12]
    copies = []
    for i in range(3):
        columns = pl.ds(128 * PARTS[i][0], 128 * PARTS[i][1])
        copies += [
            pltpu.make_async_copy(pieces[6 + i], owned.at[0, pl.ds(*ROWS[i]), :], sems.at[6 + i]),
            pltpu.make_async_copy(pieces[i], new_momentum.at[:, columns], sems.at[i]),
            pltpu.make_async_copy(pieces[3 + i], update.at[:, columns], sems.at[3 + i]),
        ]
    for copy in copies:
        copy.start()
    for copy in copies:
        copy.wait()


def body(grad, momentum, owners):
    hbm = pl.BlockSpec(memory_space=pltpu.HBM)
    vmem = pl.BlockSpec(memory_space=pltpu.VMEM)
    bf16, f32, i32 = jnp.bfloat16, jnp.float32, jnp.int32
    pieces = (
        *(jax.ShapeDtypeStruct((MATS, 128 * count), f32) for _, count in PARTS),
        *(jax.ShapeDtypeStruct((MATS, 128 * count), bf16) for _, count in PARTS),
        *(jax.ShapeDtypeStruct((count, C), bf16) for _, count in ROWS),
    )
    results = pl.pallas_call(
        kernel,
        out_shape=pieces,
        in_specs=[hbm, hbm, hbm],
        out_specs=(vmem,) * 9,
        scratch_shapes=[
            pltpu.SMEM((MATS,), i32),
            pltpu.VMEM(grad.shape, bf16),
            pltpu.VMEM(momentum.shape, f32),
            pltpu.VMEM((2, 8, 128), i32),
            pltpu.VMEM((MATS, T, 128), bf16),
            pltpu.SMEM((2, 8, 128), i32),
            pltpu.SMEM((MATS,), i32),
            pltpu.VMEM((N * T + 8, 128), f32),
            pltpu.VMEM((N, T, 128), bf16),
            pltpu.VMEM((N, T, 128), bf16),
            pltpu.VMEM((RP, C), bf16),
            pltpu.VMEM((RP, C), bf16),
            pltpu.VMEM((RP, RP), bf16),
            pltpu.VMEM((RP, RP), bf16),
            pltpu.VMEM((N, T, 128), bf16),
            pltpu.VMEM((FIXED, T, 128), bf16),
            pltpu.SemaphoreType.DMA((2 * len(PARTS) + 1,)),
            pltpu.SemaphoreType.REGULAR,
            pltpu.SemaphoreType.DMA,
            pltpu.SemaphoreType.DMA,
            pltpu.SemaphoreType.DMA,
            pltpu.SemaphoreType.DMA,
        ],
        compiler_params=pltpu.CompilerParams(
            collective_id=0, has_side_effects=True, vmem_limit_bytes=MAIN_KIB << 10
        ),
    )(owners, grad, momentum)
    return pl.pallas_call(
        write_kernel,
        out_shape=(
            jax.ShapeDtypeStruct(momentum.shape, f32),
            jax.ShapeDtypeStruct(grad.shape, bf16),
            jax.ShapeDtypeStruct((1, R, C), bf16),
        ),
        in_specs=[vmem] * 9,
        out_specs=(hbm, hbm, hbm),
        scratch_shapes=[pltpu.SemaphoreType.DMA((9,))],
        compiler_params=pltpu.CompilerParams(vmem_limit_bytes=4 << 20),
    )(*results)


def solution(mesh):
    return jax.shard_map(
        body,
        mesh=mesh,
        in_specs=(P("rep", "dp"), P("rep", "dp"), P("rep")),
        out_specs=(P("rep", "dp"), P("rep", "dp"), P(("rep", "dp"), None, None)),
        check_vma=False,
    )
```
